128 devices in a mesh: ang: 64 (over y_lo, x, z, core), row: 2 (over y_hi).
Axes of the slice: x: 4, y: 4 (y_hi: 2, y_lo: 2; y = y_hi * 2 + y_lo), z: 4, core: 2. Of those that a mesh axis runs over, the one named last changes fastest.
Arguments:
- projections: float32 [128, 128, 4096], P('ang', 'row'), may hold values from 0.05 to 1
- correlation: int32 [128], P('ang'), may hold values from 128 to 512
- offset: int32 [128], P('ang'), may hold values from 0 to 127
- smooth_taps: float32 [2, 33], replicated, may hold values from 0.2 to 1
Outputs:
- sinograms: float32 [2, 64, 128, 8192], P('row', 'ang')
The draws below stay inside these ranges and needn't reach their ends.
Inputs may be any that keep to these rules, and one draw needn't show every extreme that they name: Every offset is smaller than every correlation; correlations are at least 1.
All inputs are finite; a program needn't handle non-finite values.
Results may differ from the reference program's by a relative error of at most 0.0003.
Values sent between devices are 32-bit elements; how exact they have to be, the bound alone decides.
No kernel may reach another device: no remote copies, remote signals or barrier semaphores. Data moves between devices by JAX's collectives and lax.ppermute only.
A program may use at most 128 MiB of HBM per device.

```python
import math
import jax
import jax.numpy as jnp
from jax import lax

COLS = 4096
SMOOTH_TAPS = 33
ANGLE_TAPS = 31
NPROJ = 128
DR = 128
N_ROW = 2


def set_ends(entries, own_key, least, largest):
    dims = entries.shape
    index_at = [jax.random.randint(jax.random.fold_in(own_key, axis), (), 0, dims[axis]) for axis in range(len(dims))]
    entries = entries.at[tuple(index_at)].set(least)
    longest = dims.index(max(dims))
    index_at[longest] = (index_at[longest] + 1) % dims[longest]
    return entries.at[tuple(index_at)].set(largest)


def block_scale(stream_key, dims, cuts, low, largest):
    def one(axis_at, blocks):
        steps = jax.random.uniform(jax.random.fold_in(jax.random.fold_in(stream_key, 6), axis_at), (blocks,), jnp.float32, low / len(cuts), largest / len(cuts))
        return jnp.repeat(jnp.exp(steps), dims[axis_at] // blocks).reshape((-1,) + (1,) * (len(dims) - axis_at - 1))

    level = one(*cuts[0])
    for cut in cuts[1:]:
        level = level * one(*cut)
    return level


def setup_inputs(seed: int = 0) -> dict:
    streams_of = jax.random.split(jax.random.key(seed), 5)
    projections = jnp.clip(jnp.exp(math.log(1.0) - 2.9957323 * jax.random.uniform(streams_of[0], (NPROJ, DR, COLS), jnp.float32) ** block_scale(streams_of[0], (NPROJ, DR, COLS), ((0, 64), (1, 2)), -0.2, 0.2)), 0.05, 1.0)
    correlation = set_ends(jax.random.randint(streams_of[1], (NPROJ,), COLS // 32, COLS // 8 + 1), jax.random.fold_in(streams_of[1], 1), COLS // 32, (COLS // 8 + 1) - 1).astype(jnp.int32)
    offset = set_ends(jax.random.randint(streams_of[2], (NPROJ,), 0, COLS // 32), jax.random.fold_in(streams_of[2], 1), 0, (COLS // 32) - 1).astype(jnp.int32)
    smooth_taps = jnp.clip(jax.random.uniform(streams_of[3], (2, SMOOTH_TAPS), jnp.float32, 0.2, 1.0), 0.2, 1.0)
    return dict(projections=projections, correlation=correlation, offset=offset, smooth_taps=smooth_taps)


def stitch_one(own_image, partner, correlation_cols, lead_zeros, width):
    length = 2 * width
    column = jnp.arange(length, dtype=jnp.int32)
    placed = column - lead_zeros
    own_index = placed - width + correlation_cols
    partner_index = width - 1 - placed
    own_vals = jnp.take(own_image, jnp.clip(own_index, 0, width - 1).astype(jnp.int32), axis=1)
    partner_vals = jnp.take(partner, jnp.clip(partner_index, 0, width - 1).astype(jnp.int32), axis=1)
    weights = jnp.clip((own_index.astype(jnp.float32) + 0.5) / correlation_cols.astype(jnp.float32), 0.0, 1.0)
    intensity = weights * own_vals + (1.0 - weights) * partner_vals
    valid_mask = (placed >= 0) & (placed < length - correlation_cols)
    safe_vals = jnp.where(valid_mask, intensity, 1.0)
    return jnp.where(valid_mask, -jnp.log(safe_vals), 0.0)


def smooth_axis(field, norm_taps, axis_id):
    reach = (norm_taps.shape[0] - 1) // 2
    extent = field.shape[axis_id]
    pad_cfg = [(0, 0)] * field.ndim
    pad_cfg[axis_id] = (reach, reach)
    padded = jnp.pad(field, pad_cfg)
    total = jnp.zeros_like(field)
    for position in range(norm_taps.shape[0]):
        total = total + norm_taps[position] * lax.slice_in_dim(padded, position, position + extent, axis=axis_id)
    return total


def reference(projections, correlation, offset, smooth_taps):
    norm_taps = smooth_taps / jnp.sum(smooth_taps, axis=1, keepdims=True)

    def one_projection(proj_index):
        own_image = lax.dynamic_index_in_dim(projections, proj_index, 0, keepdims=False)
        partner = lax.dynamic_index_in_dim(projections, (proj_index + NPROJ // 2) % NPROJ, 0, keepdims=False)
        stitched = stitch_one(own_image, partner, correlation[proj_index], offset[proj_index], COLS)
        return smooth_axis(smooth_axis(stitched, norm_taps[0], 1), norm_taps[1], 0)

    smoothed = lax.map(one_projection, jnp.arange(NPROJ, dtype=jnp.int32))
    half_span = ANGLE_TAPS // 2
    length = 2 * COLS
    frequency = jnp.arange(length // 2 + 1, dtype=jnp.float32)
    ramp_gain = frequency / (length / 2)

    def one_sinogram(row_index):
        sinogram = lax.dynamic_index_in_dim(smoothed, row_index, 1, keepdims=False)
        box_sum = jnp.zeros_like(sinogram)
        for shift_by in range(-half_span, half_span + 1):
            box_sum = box_sum + jnp.roll(sinogram, shift_by, axis=0)
        highpassed = sinogram - box_sum / ANGLE_TAPS
        spectrum = jnp.fft.rfft(highpassed, axis=1)
        return jnp.fft.irfft(spectrum * ramp_gain, n=length, axis=1).astype(jnp.float32)

    filtered = lax.map(one_sinogram, jnp.arange(DR, dtype=jnp.int32))
    return filtered.reshape(N_ROW, DR // N_ROW, NPROJ, length)
```

```python
import functools
import math

import jax
import jax.numpy as jnp
import numpy as np
from jax import lax
from jax.experimental import pallas as pl
from jax.experimental.pallas import tpu as pltpu

ANGLE_TAPS = 31
LANES = 128
OUTER = 64
BLOCKS = 36
LEFT = 4
REACH = 16
TAPS = 2 * REACH + 1
LENGTH = OUTER * LANES
MIN_OVERLAP_OFFSET = 127
f32, bf16 = jnp.float32, jnp.bfloat16


def halves(x):
    high = x.astype(bf16)
    return high, (x - high.astype(f32)).astype(bf16)


def thirds(x):
    high = x.astype(bf16)
    rest = x - high.astype(f32)
    middle = rest.astype(bf16)
    return high, middle, (rest - middle.astype(f32)).astype(bf16)


def mxu(a, b):
    return jnp.dot(a, b, preferred_element_type=f32)


def source_kernel(ints, taps, own, halo, seam, seam_halo, out):
    rows = own.shape[1]
    halo_rows = halo.shape[1]
    every = rows + halo_rows
    width_blocks = own.shape[2] // LANES
    width = own.shape[2]
    row_group = ints[4]
    lane = lax.broadcasted_iota(jnp.int32, (1, LANES), 1)

    target = lax.broadcasted_iota(jnp.int32, (rows, 3 * every), 0)
    place = lax.broadcasted_iota(jnp.int32, (rows, 3 * every), 1)
    third = place // every
    source = place - third * every
    source = jnp.where((source >= rows) & (row_group > 0), source - every, source)
    tap_at = source - target + REACH
    matrix = jnp.zeros((rows, 3 * every), f32)
    for t in range(TAPS):
        matrix = jnp.where(tap_at == t, taps[1, t], matrix)
    m_high, m_mid, m_low = thirds(matrix)
    left_one = jnp.where(third == 1, m_mid.astype(f32), m_high.astype(f32)).astype(bf16)
    left_two = jnp.where(
        third == 0, m_low.astype(f32), jnp.where(third == 1, m_mid.astype(f32), m_high.astype(f32))
    ).astype(bf16)

    def smooth(pair):
        high, mid, low = thirds(pair)
        one = jnp.concatenate([high, high, mid], axis=0)
        two = jnp.concatenate([high, mid, low], axis=0)
        return mxu(left_one, one) + mxu(left_two, two)

    for s in range(2):
        overlap, lead = ints[s], ints[2 + s]
        shift = overlap - lead
        skip = shift // LANES
        turn = shift - skip * LANES
        back = lax.rem(LANES - turn, LANES)
        keep = lane < LANES - turn

        def turned(block, s=s, back=back):
            at = pl.multiple_of(jnp.clip(block, 0, width_blocks - 1) * LANES, LANES)
            both = jnp.concatenate([own[s, :, pl.ds(at, LANES)], halo[s, :, pl.ds(at, LANES)]], axis=0)
            return pltpu.roll(both, back, 1)

        def store(b, value, s=s):
            for g in range(rows // 8):
                out[pl.ds(8 * g * 2 * BLOCKS + s * BLOCKS + LEFT + b, 8, stride=2 * BLOCKS), :] = value[8 * g : 8 * g + 8]

        def finish(b, first, second, store=store):
            value = smooth(jnp.concatenate([first, second], axis=1))
            store(b, value[:, :LANES])
            return value[:, LANES:]

        mirror = (lead - 1 - lane) & (LANES - 1)
        mirror = jnp.broadcast_to(mirror, (every, LANES))
        flipped = []
        for j in range(LEFT):
            both = jnp.concatenate(
                [seam[s, :, LANES * j : LANES * (j + 1)], seam_halo[s, :, LANES * j : LANES * (j + 1)]], axis=0
            )
            flipped.append(jnp.take_along_axis(both, mirror, axis=1, mode="promise_in_bounds"))

        def blended(b, first, second):
            u = LANES * b + shift + lane
            weight = jnp.clip((u.astype(f32) + 0.5) / overlap.astype(f32), 0.0, 1.0)
            mine = jnp.where(keep, first, second)
            other = jnp.where(lane < lead, flipped[min(max(-b, 0), 3)], flipped[min(max(-b - 1, 0), 3)])
            return -jnp.log(weight * mine + (1.0 - weight) * other)

        for b in range(-LEFT, 2, 2):
            parts = [turned(b + skip + i) for i in range(3)]
            store(b + 1, finish(b, blended(b, parts[0], parts[1]), blended(b + 1, parts[1], parts[2])))

        def plain(b, first, second):
            u = LANES * b + shift + lane
            return -jnp.log(jnp.where(u < width, jnp.where(keep, first, second), 1.0))

        def pair(i, carry):
            b = 2 * i
            parts = [turned(b + skip + j) for j in range(3)]
            value = finish(b, plain(b, parts[0], parts[1]), plain(b + 1, parts[1], parts[2]))
            last = b + 1 == width_blocks - 1
            value = jnp.where(last & (lane == LANES - 1), shift.astype(f32), value)
            value = jnp.where(last & (lane == LANES - 2) & (shift > 1), lead.astype(f32), value)
            store(b + 1, value)
            return carry

        lax.fori_loop(1, width_blocks // 2, pair, 0)


def times(a, b):
    return (a[0] * b[0] - a[1] * b[1], a[0] * b[1] + a[1] * b[0])


def dft(x, sign):
    n = len(x)
    if n == 1:
        return x
    even, odd = dft(x[0::2], sign), dft(x[1::2], sign)
    root = math.sqrt(0.5)
    first, second = [], []
    for k in range(n // 2):
        re, im = odd[k]
        if 4 * k == n:
            re, im = -sign * im, sign * re
        elif 8 * k == n:
            re, im = root * (re - sign * im), root * (im + sign * re)
        elif 8 * k == 3 * n:
            re, im = root * (-re - sign * im), root * (-im + sign * re)
        first.append((even[k][0] + re, even[k][1] + im))
        second.append((even[k][0] - re, even[k][1] - im))
    return first + second


def small_twist(value, power, sign):
    if power % OUTER == 0:
        return value
    angle = sign * 2.0 * math.pi * (power % OUTER) / OUTER
    return times(value, (np.float32(math.cos(angle)), np.float32(math.sin(angle))))


def sinogram_kernel(
    x, gain_re, gain_im, ramp, ends, twist_re, twist_im, end_u, end_v, box, forward, backward, end_w,
    out, field, mid_re, mid_im, rows, end_rows,
):
    half = out.shape[0] // 2
    lane = lax.broadcasted_iota(jnp.int32, (8, LANES), 1)

    def place(g, carry):
        sides = []
        for side in range(2):
            start = (side * half + 8 * g) * BLOCKS
            blocks = [x[pl.ds(start + k, 8, stride=BLOCKS), :] for k in range(BLOCKS)]
            last = blocks[-1]
            shift = last[:, LANES - 1 :]
            lead = jnp.where(shift > 1.5, last[:, LANES - 2 : LANES - 1], float(MIN_OVERLAP_OFFSET))
            hidden = (lane == LANES - 1) | ((lane == LANES - 2) & (shift > 1.5))
            blocks[-1] = jnp.where(hidden, 0.0, last)
            sides.append((blocks, shift.astype(jnp.int32), lead.astype(jnp.int32)))
        for side in range(2):
            mine, _, lead = sides[side]
            theirs, their_shift, _ = sides[1 - side]
            at = pl.ds(pl.multiple_of(side * half + 8 * g, 8), 8)
            spot = LANES - 1 + lead - their_shift - lane
            index = spot & (LANES - 1)
            jump = (spot >> 7) + 4
            mirrored = {}
            for k in range(OUTER // 2):
                mirrored[k] = jnp.take_along_axis(theirs[LEFT + k], index, axis=1, mode="promise_in_bounds")
            mirrored[-1] = mirrored[0]
            mirrored[OUTER // 2] = jnp.zeros((8, LANES), f32)
            for step in (1, 2, 4):
                moved = (jump & step) != 0
                top = OUTER // 2
                mirrored = {
                    k: jnp.where(moved, mirrored[min(k + step, top)], mirrored[k]) for k in mirrored
                }
            for c in range(OUTER // 2 - LEFT + 1):
                value = mirrored[OUTER // 2 - 5 - c]
                if c == OUTER // 2 - LEFT:
                    value = jnp.where(lane >= lead, mine[0], value)
                field[c, at, :] = value
            for k in range(1, BLOCKS):
                field[OUTER // 2 - LEFT + k, at, :] = mine[k]
        return carry

    lax.fori_loop(0, half // 8, place, 0)

    def highpass(i, carry):
        both = jnp.concatenate([field[2 * i], field[2 * i + 1]], axis=1)
        high, low = halves(both)
        sums = mxu(box[...], jnp.concatenate([high, low], axis=0))
        both = both - sums * np.float32(1.0 / ANGLE_TAPS)
        field[2 * i] = both[:, :LANES]
        field[2 * i + 1] = both[:, LANES:]
        return carry

    lax.fori_loop(0, OUTER // 2, highpass, 0)

    border = jnp.concatenate(
        [field[0, :half], field[0, half:], field[OUTER - 1, :half], field[OUTER - 1, half:]], axis=1
    )
    end_rows[...] = jnp.dot(border, ends[...], precision=lax.Precision.HIGHEST, preferred_element_type=f32)

    def filtered(g, carry):
        low_at = pl.ds(pl.multiple_of(8 * g, 8), 8)
        high_at = pl.ds(pl.multiple_of(half + 8 * g, 8), 8)
        for b in range(8):
            got = dft([(field[8 * a + b, low_at, :], field[8 * a + b, high_at, :]) for a in range(8)], -1.0)
            for d in range(8):
                mid_re[8 * d + b], mid_im[8 * d + b] = small_twist(got[d], d * b, -1.0)
        for d in range(8):
            got = dft([(mid_re[8 * d + b], mid_im[8 * d + b]) for b in range(8)], -1.0)
            for e in range(8):
                k = d + 8 * e
                re, im = times(got[e], (twist_re[k : k + 1, :], twist_im[k : k + 1, :]))
                rows[k, :, :LANES] = re
                rows[k, :, LANES:] = im
        for part in range(2):
            n = OUTER // 2
            span = slice(part * n, (part + 1) * n)
            high, low = halves(rows[span].reshape(n * 8, 2 * LANES))
            spectrum = mxu(high, forward[0]) + mxu(low, forward[0]) + mxu(high, forward[1])
            spectrum = spectrum.reshape(n, 8, 2 * LANES)
            here = end_rows[low_at, :]
            tail = here[None, :, :LANES] * end_u[span][:, None, :] + here[None, :, LANES:] * end_v[span][:, None, :]
            tail = tail.reshape(n * 8, LANES)
            t_high = tail.astype(bf16).astype(f32)
            front = lax.broadcasted_iota(jnp.int32, (1, LANES), 1) < LANES // 2
            t_one = jnp.where(front, t_high, tail - t_high).astype(bf16)
            t_two = jnp.where(front, t_high, 0.0).astype(bf16)
            wrapped = mxu(jnp.concatenate([t_one, t_two], axis=1), end_w[...]).reshape(n, 8, 2 * LANES)
            g_re, g_im, r = gain_re[span][:, None, :], gain_im[span][:, None, :], ramp[span][:, None, :]
            re, im = times((spectrum[..., :LANES], spectrum[..., LANES:]), (g_re, g_im))
            re = re - r * wrapped[..., :LANES]
            im = im - r * wrapped[..., LANES:]
            high, low = halves(jnp.concatenate([re, im], axis=2).reshape(n * 8, 2 * LANES))
            signal = mxu(high, backward[0]) + mxu(low, backward[0]) + mxu(high, backward[1])
            signal = signal.reshape(n, 8, 2 * LANES)
            re, im = times(
                (signal[..., :LANES], signal[..., LANES:]), (twist_re[span][:, None, :], -twist_im[span][:, None, :])
            )
            rows[span, :, :LANES] = re
            rows[span, :, LANES:] = im
        for d in range(8):
            got = dft([(rows[d + 8 * e, :, :LANES], rows[d + 8 * e, :, LANES:]) for e in range(8)], 1.0)
            for b in range(8):
                mid_re[8 * d + b], mid_im[8 * d + b] = small_twist(got[b], d * b, 1.0)
        for b in range(8):
            got = dft([(mid_re[8 * d + b], mid_im[8 * d + b]) for d in range(8)], 1.0)
            for a in range(8):
                c = 8 * a + b
                out[low_at, c * LANES : (c + 1) * LANES] = got[a][0]
                out[high_at, c * LANES : (c + 1) * LANES] = got[a][1]
        return carry

    lax.fori_loop(0, half // 8, filtered, 0)


@functools.lru_cache(maxsize=None)
def tables(nproj):
    k1 = np.arange(OUTER)[:, None]
    l = np.arange(LANES)[None, :]
    angle = 2.0 * np.pi * (k1 * l % LENGTH) / LENGTH
    table = dict(twist_re=np.cos(angle), twist_im=-np.sin(angle))
    inner = 2.0 * np.pi * (np.arange(LANES)[:, None] * l % LANES) / LANES
    cos, sin = np.cos(inner), np.sin(inner)
    forward = np.block([[cos, -sin], [sin, cos]])
    backward = np.block([[cos, sin], [-sin, cos]])

    def two(w):
        high = w.astype(np.float32).astype(jnp.bfloat16)
        low = (w - high.astype(np.float64)).astype(np.float32).astype(jnp.bfloat16)
        return high, low

    table["forward"] = np.stack(two(forward))
    table["backward"] = np.stack(two(backward))
    columns = np.concatenate([np.arange(REACH), LENGTH - REACH + np.arange(REACH)])
    some = columns % LANES
    end_w = np.concatenate([forward[some], forward[LANES + some]], axis=0)
    high, low = two(end_w)
    table["end_w"] = np.concatenate([high, high, low, np.zeros_like(low)], axis=0)
    theta = 2.0 * np.pi * (k1 * columns[None, :] % LENGTH) / LENGTH
    table["end_u"] = np.tile(np.cos(theta), (1, 4))
    table["end_v"] = np.tile(np.concatenate([np.sin(theta), -np.sin(theta)], axis=1), (1, 2))
    tap_at = np.full((4, LANES, 2, 4, 2 * REACH), -1, np.int32)
    for i in range(REACH):
        for arrangement in range(2):
            for group in range(4):
                part = (group + arrangement) % 2
                for t in range(TAPS):
                    if LANES - REACH + i + t < LANES:
                        tap_at[2 + part, LANES - REACH + i + t, arrangement, group, i] = t
                    if i + t - 2 * REACH >= 0:
                        tap_at[part, i + t - 2 * REACH, arrangement, group, REACH + i] = t
    table["tap_at"] = tap_at.reshape(4 * LANES, 2 * LANES)
    frequency = k1 + OUTER * l
    table["ramp"] = np.minimum(frequency, LENGTH - frequency) / (LENGTH / 2) / LENGTH
    lag = np.arange(TAPS) - REACH
    a = 2.0 * np.pi * (k1 * lag[None, :] % LENGTH) / LENGTH
    b = 2.0 * np.pi * (lag[:, None] * l % LANES) / LANES
    table["gain_left"] = np.stack(
        [np.concatenate([np.cos(a), -np.sin(a)], axis=1), np.concatenate([np.sin(a), np.cos(a)], axis=1)]
    )
    table["gain_right"] = np.concatenate([np.cos(b), np.sin(b)], axis=0)
    p = np.arange(nproj)
    gap = (p[:, None] - p[None, :]) % nproj
    near = (np.minimum(gap, nproj - gap) <= ANGLE_TAPS // 2).astype(np.float32).astype(jnp.bfloat16)
    table["box"] = np.concatenate([near, near], axis=1)
    return {k: v.astype(np.float32) if v.dtype == np.float64 else v for k, v in table.items()}


def vmem_spec():
    return pl.BlockSpec(memory_space=pltpu.VMEM)


def smem_spec():
    return pl.BlockSpec(memory_space=pltpu.SMEM)


def local(projections, correlation, offset, smooth_taps):
    ang, row = lax.axis_size("ang"), lax.axis_size("row")
    here = lax.axis_index("row")
    per, rows, width = projections.shape
    nproj = per * ang
    seam_cols = LEFT * LANES

    halo = jnp.where(here == 0, projections[:, rows - REACH :], projections[:, :REACH])
    half_turn = [(i, (i + ang // 2) % ang) for i in range(ang)]
    across = [(i, 1 - i) for i in range(row)]
    both = [(a * row + r, b * row + s) for a, b in half_turn for r, s in across]
    seam_halo = lax.ppermute(halo[:, :, :seam_cols], ("ang", "row"), both)
    seam = lax.ppermute(projections[:, :, :seam_cols], "ang", half_turn)
    halo = lax.ppermute(halo, "row", across)

    taps = smooth_taps / jnp.sum(smooth_taps, axis=1, keepdims=True)
    ints = jnp.concatenate([correlation, offset, here[None].astype(jnp.int32)])
    sent = pl.pallas_call(
        source_kernel,
        out_shape=jax.ShapeDtypeStruct((rows * per * BLOCKS, LANES), f32),
        in_specs=[smem_spec(), smem_spec()] + [vmem_spec()] * 4,
        out_specs=vmem_spec(),
        compiler_params=pltpu.CompilerParams(vmem_limit_bytes=40 * 1024 * 1024),
        name="source",
    )(ints, taps, projections, halo, seam, seam_halo)

    got = lax.all_to_all(sent.reshape(rows, per * BLOCKS, LANES), "ang", split_axis=0, concat_axis=0, tiled=True)
    got = got.reshape(nproj * BLOCKS, LANES)

    t = tables(nproj)
    left = (t["gain_left"] * jnp.tile(taps[0], 2)).reshape(2 * OUTER, 2 * TAPS)
    gain = jnp.dot(left, t["gain_right"], precision=lax.Precision.HIGHEST) * jnp.tile(t["ramp"], (2, 1))
    ends = jnp.zeros(t["tap_at"].shape, f32)
    for k in range(TAPS):
        ends = jnp.where(t["tap_at"] == k, taps[0, k], ends)

    out = pl.pallas_call(
        sinogram_kernel,
        out_shape=jax.ShapeDtypeStruct((nproj, LENGTH), f32),
        in_specs=[vmem_spec()] * 13,
        out_specs=vmem_spec(),
        scratch_shapes=[
            pltpu.VMEM((OUTER, nproj, LANES), f32),
            pltpu.VMEM((OUTER, 8, LANES), f32),
            pltpu.VMEM((OUTER, 8, LANES), f32),
            pltpu.VMEM((OUTER, 8, 2 * LANES), f32),
            pltpu.VMEM((nproj // 2, 2 * LANES), f32),
        ],
        compiler_params=pltpu.CompilerParams(vmem_limit_bytes=56 * 1024 * 1024),
        name="sinogram",
    )(
        got, gain[:OUTER], gain[OUTER:], t["ramp"], ends, t["twist_re"], t["twist_im"], t["end_u"], t["end_v"],
        t["box"], t["forward"], t["backward"], t["end_w"],
    )
    return out[None, None]


def solution(mesh):
    P = jax.sharding.PartitionSpec
    placed = (P("ang", "row", None), P("ang"), P("ang"), P())
    return jax.shard_map(
        local, mesh=mesh, in_specs=placed, out_specs=P("row", "ang", None, None), check_vma=False
    )
```

```python
import functools
import math

import jax
import jax.numpy as jnp
import numpy as np
from jax import lax
from jax.experimental import pallas as pl
from jax.experimental.pallas import tpu as pltpu

ANGLE_TAPS = 31
LANES = 128
OUTER = 64
BLOCKS = 36
LEFT = 4
REACH = 16
TAPS = 2 * REACH + 1
LENGTH = OUTER * LANES
MIN_OVERLAP_OFFSET = 127
TOGETHER = 2
f32, bf16 = jnp.float32, jnp.bfloat16


def halves(x):
    high = x.astype(bf16)
    return high, (x - high.astype(f32)).astype(bf16)


def thirds(x):
    high = x.astype(bf16)
    rest = x - high.astype(f32)
    middle = rest.astype(bf16)
    return high, middle, (rest - middle.astype(f32)).astype(bf16)


def mxu(a, b):
    return jnp.dot(a, b, preferred_element_type=f32)


def row_matrices(taps, rows, sources, place_of):
    target = lax.broadcasted_iota(jnp.int32, (rows, 3 * sources), 0)
    at = lax.broadcasted_iota(jnp.int32, (rows, 3 * sources), 1)
    third = at // sources
    tap_at = place_of(at - third * sources) - target + REACH
    matrix = jnp.zeros((rows, 3 * sources), f32)
    for t in range(TAPS):
        matrix = jnp.where(tap_at == t, taps[1, t], matrix)
    high, mid, low = (part.astype(f32) for part in thirds(matrix))
    one = jnp.where(third == 1, mid, high).astype(bf16)
    two = jnp.where(third == 0, low, jnp.where(third == 1, mid, high)).astype(bf16)
    return one, two


def row_filter(matrices, field):
    high, mid, low = thirds(field)
    one = jnp.concatenate([high, high, mid], axis=0)
    two = jnp.concatenate([high, mid, low], axis=0)
    return mxu(matrices[0], one) + mxu(matrices[1], two)


def block_of(refs, s, block):
    last = refs[0].shape[2] // LANES - 1
    at = jnp.clip(block, 0, last) * LANES
    if not isinstance(at, int):
        at = pl.multiple_of(at, LANES)
    parts = [ref[s, :, pl.ds(at, LANES)] for ref in refs]
    return parts[0] if len(parts) == 1 else jnp.concatenate(parts, axis=0)


class Shifted:
    def __init__(self, ints, s, refs):
        self.overlap, self.lead = ints[s], ints[2 + s]
        self.shift = self.overlap - self.lead
        self.skip = self.shift // LANES
        turn = self.shift - self.skip * LANES
        self.back = lax.rem(LANES - turn, LANES)
        self.lane = lax.broadcasted_iota(jnp.int32, (1, LANES), 1)
        self.keep = self.lane < LANES - turn
        self.s, self.refs = s, refs

    def turned(self, block):
        return pltpu.roll(block_of(self.refs, self.s, block + self.skip), self.back, 1)

    def column(self, b):
        return LANES * b + self.shift + self.lane

    def plain_pair(self, b, width):
        parts = [self.turned(b + j) for j in range(3)]
        logs = []
        for j in range(2):
            value = jnp.where(self.keep, parts[j], parts[j + 1])
            logs.append(-jnp.log(jnp.where(self.column(b + j) < width, value, 1.0)))
        return jnp.concatenate(logs, axis=1)


def early_kernel(ints, taps, own, out):
    rows, width = own.shape[1], own.shape[2]
    matrices = row_matrices(taps, rows, rows, lambda at: at)
    for s in range(2):
        moved = Shifted(ints, s, [own])

        def pair(i, carry, s=s, moved=moved):
            at = pl.ds(pl.multiple_of((i - 1) * 2 * LANES, 2 * LANES), 2 * LANES)
            out[s, :, at] = row_filter(matrices, moved.plain_pair(2 * i, width))
            return carry

        lax.fori_loop(1, width // LANES // 2, pair, 0, unroll=3)


def source_kernel(ints, taps, early, own, halo, seam, seam_halo, out):
    rows, halo_rows, width = own.shape[1], halo.shape[1], halo.shape[2]
    every = rows + halo_rows
    row_group = ints[4]
    lane = lax.broadcasted_iota(jnp.int32, (1, LANES), 1)

    def across(at):
        return jnp.where((at >= rows) & (row_group > 0), at - every, at)

    matrices = row_matrices(taps, rows, every, across)
    halo_matrices = row_matrices(taps, rows, halo_rows, lambda at: across(at + rows))

    for s in range(2):

        def store(b, value, s=s):
            for g in range(rows // 8):
                at = pl.ds(8 * g * 2 * BLOCKS + s * BLOCKS + LEFT + b, 8, stride=2 * BLOCKS)
                out[at, :] = value[8 * g : 8 * g + 8]

        moved = Shifted(ints, s, [own, halo.at[:, :, : own.shape[2]]])
        overlap, lead, shift = moved.overlap, moved.lead, moved.shift
        mirror = jnp.broadcast_to((lead - 1 - lane) & (LANES - 1), (every, LANES))
        flipped = [
            jnp.take_along_axis(block_of([seam, seam_halo], s, j), mirror, axis=1, mode="promise_in_bounds")
            for j in range(LEFT)
        ]

        def blended(b, first, second):
            weight = jnp.clip((moved.column(b).astype(f32) + 0.5) / overlap.astype(f32), 0.0, 1.0)
            mine = jnp.where(moved.keep, first, second)
            other = jnp.where(lane < lead, flipped[min(max(-b, 0), 3)], flipped[min(max(-b - 1, 0), 3)])
            return -jnp.log(weight * mine + (1.0 - weight) * other)

        for b in range(-LEFT, 2, 2):
            parts = [moved.turned(b + i) for i in range(3)]
            logs = [blended(b + i, parts[i], parts[i + 1]) for i in range(2)]
            value = row_filter(matrices, jnp.concatenate(logs, axis=1))
            store(b, value[:, :LANES])
            store(b + 1, value[:, LANES:])

        rest = Shifted(ints, s, [halo])

        def pair(i, carry, s=s, store=store, rest=rest):
            b = 2 * i
            at = pl.ds(pl.multiple_of((b - 2) * LANES, 2 * LANES), 2 * LANES)
            value = early[s, :, at] + row_filter(halo_matrices, rest.plain_pair(b, width))
            store(b, value[:, :LANES])
            value = value[:, LANES:]
            last = b + 2 == width // LANES
            value = jnp.where(last & (lane == LANES - 1), rest.shift.astype(f32), value)
            value = jnp.where(last & (lane == LANES - 2) & (rest.shift > 1), rest.lead.astype(f32), value)
            store(b + 1, value)
            return carry

        lax.fori_loop(1, width // LANES // 2, pair, 0, unroll=15)


def times(a, b):
    return (a[0] * b[0] - a[1] * b[1], a[0] * b[1] + a[1] * b[0])


def dft(x, sign):
    n = len(x)
    if n == 1:
        return x
    even, odd = dft(x[0::2], sign), dft(x[1::2], sign)
    root = math.sqrt(0.5)
    first, second = [], []
    for k in range(n // 2):
        re, im = odd[k]
        if 4 * k == n:
            re, im = -sign * im, sign * re
        elif 8 * k == n:
            re, im = root * (re - sign * im), root * (im + sign * re)
        elif 8 * k == 3 * n:
            re, im = root * (-re - sign * im), root * (-im + sign * re)
        first.append((even[k][0] + re, even[k][1] + im))
        second.append((even[k][0] - re, even[k][1] - im))
    return first + second


def small_twist(value, power, sign):
    if power % OUTER == 0:
        return value
    angle = sign * 2.0 * math.pi * (power % OUTER) / OUTER
    return times(value, (np.float32(math.cos(angle)), np.float32(math.sin(angle))))


def sinogram_kernel(
    x, table, weights, out_hbm, out, field, mid_re, mid_im, rows, end_rows, sent
):
    gain_re, gain_im, twist_re, twist_im, end_u, end_v, ramp, _ = (
        table.at[OUTER * (k // 2) : OUTER * (k // 2 + 1), LANES * (k % 2) : LANES * (k % 2 + 1)] for k in range(8)
    )
    box = weights.at[: 2 * OUTER]
    forward, backward = ([weights.at[(at + k) * 2 * LANES - LANES : (at + k + 1) * 2 * LANES - LANES] for k in range(2)] for at in (1, 3))
    end_w = weights.at[5 * 2 * LANES - LANES :]
    half = out.shape[0] // 2
    lane = lax.broadcasted_iota(jnp.int32, (8, LANES), 1)

    def place(g, carry):
        sides = []
        for side in range(2):
            start = (side * half + 8 * g) * BLOCKS
            blocks = [x[pl.ds(start + k, 8, stride=BLOCKS), :] for k in range(BLOCKS)]
            last = blocks[-1]
            shift = last[:, LANES - 1 :]
            lead = jnp.where(shift > 1.5, last[:, LANES - 2 : LANES - 1], float(MIN_OVERLAP_OFFSET))
            hidden = (lane == LANES - 1) | ((lane == LANES - 2) & (shift > 1.5))
            blocks[-1] = jnp.where(hidden, 0.0, last)
            sides.append((blocks, shift.astype(jnp.int32), lead.astype(jnp.int32)))
        for side in range(2):
            mine, _, lead = sides[side]
            theirs, their_shift, _ = sides[1 - side]
            at = pl.ds(pl.multiple_of(side * half + 8 * g, 8), 8)
            spot = LANES - 1 + lead - their_shift - lane
            index = spot & (LANES - 1)
            jump = (spot >> 7) + 4
            mirrored = {}
            for k in range(OUTER // 2):
                mirrored[k] = jnp.take_along_axis(theirs[LEFT + k], index, axis=1, mode="promise_in_bounds")
            mirrored[-1] = mirrored[0]
            mirrored[OUTER // 2] = jnp.zeros((8, LANES), f32)
            for step in (1, 2, 4):
                moved = (jump & step) != 0
                top = OUTER // 2
                mirrored = {
                    k: jnp.where(moved, mirrored[min(k + step, top)], mirrored[k]) for k in mirrored
                }
            for c in range(OUTER // 2 - LEFT + 1):
                value = mirrored[OUTER // 2 - 5 - c]
                if c == OUTER // 2 - LEFT:
                    value = jnp.where(lane >= lead, mine[0], value)
                field[c, at, :] = value
            for k in range(1, BLOCKS):
                field[OUTER // 2 - LEFT + k, at, :] = mine[k]
        return carry

    lax.fori_loop(0, half // 8, place, 0)

    def highpass(i, carry):
        both = jnp.concatenate([field[2 * i], field[2 * i + 1]], axis=1)
        high, low = halves(both)
        sums = mxu(box[...], jnp.concatenate([high, low], axis=0))
        both = both - sums * np.float32(1.0 / ANGLE_TAPS)
        field[2 * i] = both[:, :LANES]
        field[2 * i + 1] = both[:, LANES:]
        return carry

    lax.fori_loop(0, OUTER // 2, highpass, 0, unroll=8)

    edge = lax.broadcasted_iota(jnp.int32, (1, LANES), 1) < LANES // 2
    border = [jnp.where(edge, field[0, at : at + half], field[OUTER - 1, at : at + half]) for at in (0, half)]
    tail_of = [table[4 * OUTER :, LANES * k : LANES * (k + 1)] for k in range(2)]
    tails = jnp.dot(border[0], tail_of[0], precision=lax.Precision.HIGHEST, preferred_element_type=f32)
    tails += jnp.dot(border[1], tail_of[1], precision=lax.Precision.HIGHEST, preferred_element_type=f32)
    end_rows[:, :LANES] = tails
    end_rows[:, LANES:] = pltpu.roll(tails, 2 * REACH, 1)

    def outer_forward(low_at, high_at, mid_re, mid_im, rows):
        for b in range(8):
            got = dft([(field[8 * a + b, low_at, :], field[8 * a + b, high_at, :]) for a in range(8)], -1.0)
            for d in range(8):
                mid_re[8 * d + b], mid_im[8 * d + b] = small_twist(got[d], d * b, -1.0)
        for d in range(8):
            got = dft([(mid_re[8 * d + b], mid_im[8 * d + b]) for b in range(8)], -1.0)
            for e in range(8):
                k = d + 8 * e
                re, im = times(got[e], (twist_re[k : k + 1, :], twist_im[k : k + 1, :]))
                rows[k, :, :LANES] = re
                rows[k, :, LANES:] = im

    def inner(low_at, rows):
        for part in range(2):
            n = OUTER // 2
            span = slice(part * n, (part + 1) * n)
            high, low = halves(rows[span].reshape(n * 8, 2 * LANES))
            spectrum = mxu(high, forward[0][...]) + mxu(low, forward[0][...]) + mxu(high, forward[1][...])
            spectrum = spectrum.reshape(n, 8, 2 * LANES)
            here = end_rows[low_at, :]
            tail = here[None, :, :LANES] * end_u[span][:, None, :] + here[None, :, LANES:] * end_v[span][:, None, :]
            tail = tail.reshape(n * 8, LANES)
            t_high = tail.astype(bf16).astype(f32)
            front = lax.broadcasted_iota(jnp.int32, (1, LANES), 1) < LANES // 2
            t_one = jnp.where(front, t_high, tail - t_high).astype(bf16)
            t_two = jnp.where(front, t_high, 0.0).astype(bf16)
            wrapped = mxu(jnp.concatenate([t_one, t_two], axis=1), end_w[...]).reshape(n, 8, 2 * LANES)
            g_re, g_im, r = gain_re[span][:, None, :], gain_im[span][:, None, :], ramp[span][:, None, :]
            re, im = times((spectrum[..., :LANES], spectrum[..., LANES:]), (g_re, g_im))
            re = re - r * wrapped[..., :LANES]
            im = im - r * wrapped[..., LANES:]
            high, low = halves(jnp.concatenate([re, im], axis=2).reshape(n * 8, 2 * LANES))
            signal = mxu(high, backward[0][...]) + mxu(low, backward[0][...]) + mxu(high, backward[1][...])
            signal = signal.reshape(n, 8, 2 * LANES)
            re, im = times(
                (signal[..., :LANES], signal[..., LANES:]), (twist_re[span][:, None, :], -twist_im[span][:, None, :])
            )
            rows[span, :, :LANES] = re
            rows[span, :, LANES:] = im

    def outer_backward(low_at, high_at, mid_re, mid_im, rows):
        for d in range(8):
            got = dft([(rows[d + 8 * e, :, :LANES], rows[d + 8 * e, :, LANES:]) for e in range(8)], 1.0)
            for b in range(8):
                mid_re[8 * d + b], mid_im[8 * d + b] = small_twist(got[b], d * b, 1.0)
        for b in range(8):
            got = dft([(mid_re[8 * d + b], mid_im[8 * d + b]) for d in range(8)], 1.0)
            for a in range(8):
                c = 8 * a + b
                out[low_at, c * LANES : (c + 1) * LANES] = got[a][0]
                out[high_at, c * LANES : (c + 1) * LANES] = got[a][1]

    def copies(g):
        for side in range(2):
            at = pl.ds(pl.multiple_of(side * half + 8 * g, 8), 8)
            yield pltpu.make_async_copy(out.at[at], out_hbm.at[at], sent.at[side, g])

    def filtered(i, carry):
        spots = []
        for j in range(TOGETHER):
            g = TOGETHER * i + j
            low_at = pl.ds(pl.multiple_of(8 * g, 8), 8)
            high_at = pl.ds(pl.multiple_of(half + 8 * g, 8), 8)
            spots.append((low_at, high_at, mid_re.at[j], mid_im.at[j], rows.at[j]))
        for spot in spots:
            outer_forward(*spot)
        for spot in spots:
            inner(spot[0], spot[4])
        for spot in spots:
            outer_backward(*spot)
        for j in range(TOGETHER):
            for copy in copies(TOGETHER * i + j):
                copy.start()
        return carry

    lax.fori_loop(0, half // 8 // TOGETHER, filtered, 0)
    for g in range(half // 8):
        for copy in copies(g):
            copy.wait()


@functools.lru_cache(maxsize=None)
def tables(nproj):
    k1 = np.arange(OUTER)[:, None]
    l = np.arange(LANES)[None, :]
    angle = 2.0 * np.pi * (k1 * l % LENGTH) / LENGTH
    table = dict(twist_re=np.cos(angle), twist_im=-np.sin(angle))
    inner = 2.0 * np.pi * (np.arange(LANES)[:, None] * l % LANES) / LANES
    cos, sin = np.cos(inner), np.sin(inner)
    forward = np.block([[cos, -sin], [sin, cos]])
    backward = np.block([[cos, sin], [-sin, cos]])

    def two(w):
        high = w.astype(np.float32).astype(jnp.bfloat16)
        low = (w - high.astype(np.float64)).astype(np.float32).astype(jnp.bfloat16)
        return high, low

    table["forward"] = np.stack(two(forward))
    table["backward"] = np.stack(two(backward))
    columns = np.concatenate([np.arange(REACH), LENGTH - REACH + np.arange(REACH)])
    some = columns % LANES
    end_w = np.concatenate([forward[some], forward[LANES + some]], axis=0)
    high, low = two(end_w)
    table["end_w"] = np.concatenate([high, high, low, np.zeros_like(low)], axis=0)
    theta = 2.0 * np.pi * (k1 * columns[None, :] % LENGTH) / LENGTH
    table["end_u"] = np.tile(np.cos(theta), (1, 4))
    table["end_v"] = np.tile(np.concatenate([np.sin(theta), -np.sin(theta)], axis=1), (1, 2))
    tap_at = np.full((LANES, 2, 4, 2 * REACH), -1, np.int32)
    for i in range(REACH):
        for group in range(4):
            for t in range(TAPS):
                if LANES - REACH + i + t < LANES:
                    tap_at[LANES - REACH + i + t, group % 2, group, i] = t
                if i + t - 2 * REACH >= 0:
                    tap_at[i + t - 2 * REACH, group % 2, group, REACH + i] = t
    table["tap_at"] = tap_at.reshape(LANES, 2 * LANES)
    frequency = k1 + OUTER * l
    table["ramp"] = np.minimum(frequency, LENGTH - frequency) / (LENGTH / 2) / LENGTH
    lag = np.arange(TAPS) - REACH
    a = 2.0 * np.pi * (k1 * lag[None, :] % LENGTH) / LENGTH
    b = 2.0 * np.pi * (lag[:, None] * l % LANES) / LANES
    table["gain_left"] = np.stack(
        [np.concatenate([np.cos(a), -np.sin(a)], axis=1), np.concatenate([np.sin(a), np.cos(a)], axis=1)]
    )
    table["gain_right"] = np.concatenate([np.cos(b), np.sin(b)], axis=0)
    p = np.arange(nproj)
    gap = (p[:, None] - p[None, :]) % nproj
    near = (np.minimum(gap, nproj - gap) <= ANGLE_TAPS // 2).astype(np.float32).astype(jnp.bfloat16)
    table["box"] = np.concatenate([near, near], axis=1)
    pairs = (("twist_re", "twist_im"), ("end_u", "end_v"), ("ramp", "ramp"))
    fixed = np.block([[table[k] for k in pair] for pair in pairs]).astype(np.float32)
    weights = np.concatenate([table["box"], *table["forward"], *table["backward"], table["end_w"]], axis=0)
    gain = [table[k].astype(np.float32) for k in ("gain_left", "gain_right")]
    return fixed, weights, gain, table["tap_at"]


def vmem_spec():
    return pl.BlockSpec(memory_space=pltpu.VMEM)


def hbm_spec():
    return pl.BlockSpec(memory_space=pltpu.MemorySpace.HBM)


def smem_spec():
    return pl.BlockSpec(memory_space=pltpu.SMEM)


def early_side(ints, taps, projections):
    per, rows, width = projections.shape
    shape = jax.ShapeDtypeStruct((per, rows, width - 2 * LANES), f32)
    return pl.pallas_call(
        early_kernel,
        out_shape=shape,
        in_specs=[smem_spec(), smem_spec(), vmem_spec()],
        out_specs=vmem_spec(),
        compiler_params=pltpu.CompilerParams(vmem_limit_bytes=24 * 1024 * 1024),
        cost_estimate=pl.CostEstimate(flops=12 * per * rows * rows * width, bytes_accessed=8 * per * rows * width, transcendentals=per * rows * width),
        name="early",
    )(ints, taps, projections)


def source_side(ints, taps, early, projections, halo, seam, seam_halo):
    per, rows, _ = projections.shape
    return pl.pallas_call(
        source_kernel,
        grid=(1,),
        out_shape=jax.ShapeDtypeStruct((rows * per * BLOCKS, LANES), f32),
        in_specs=[smem_spec(), smem_spec(), vmem_spec(), pl.BlockSpec((per, rows, 8 * LANES), lambda i: (0, 0, 0))]
        + [vmem_spec()] * 3,
        out_specs=vmem_spec(),
        compiler_params=pltpu.CompilerParams(vmem_limit_bytes=24 * 1024 * 1024),
        name="source",
    )(ints, taps, early, projections, halo, seam, seam_halo)


def sinogram_side(got, taps):
    nproj = got.shape[0] // BLOCKS
    fixed, weights, (gain_left, gain_right), tap_at = tables(nproj)
    left = (gain_left * jnp.tile(taps[0], 2)).reshape(2 * OUTER, 2 * TAPS)
    gain = jnp.dot(left, gain_right, precision=lax.Precision.HIGHEST) * jnp.tile(fixed[2 * OUTER :, :LANES], (2, 1))
    ends = jnp.zeros(tap_at.shape, f32)
    for k in range(TAPS):
        ends = jnp.where(tap_at == k, taps[0, k], ends)
    table = jnp.concatenate([jnp.concatenate([gain[:OUTER], gain[OUTER:]], axis=1), fixed, ends], axis=0)
    return pl.pallas_call(
        sinogram_kernel,
        out_shape=jax.ShapeDtypeStruct((nproj, LENGTH), f32),
        in_specs=[vmem_spec()] * 3,
        out_specs=hbm_spec(),
        scratch_shapes=[
            pltpu.VMEM((nproj, LENGTH), f32),
            pltpu.VMEM((OUTER, nproj, LANES), f32),
            pltpu.VMEM((TOGETHER, OUTER, 8, LANES), f32),
            pltpu.VMEM((TOGETHER, OUTER, 8, LANES), f32),
            pltpu.VMEM((TOGETHER, OUTER, 8, 2 * LANES), f32),
            pltpu.VMEM((nproj // 2, 2 * LANES), f32),
            pltpu.SemaphoreType.DMA((2, nproj // 16)),
        ],
        compiler_params=pltpu.CompilerParams(vmem_limit_bytes=28 * 1024 * 1024),
        name="sinogram",
    )(got, table, jnp.asarray(weights))


def local(projections, correlation, offset, smooth_taps):
    ang, row = lax.axis_size("ang"), lax.axis_size("row")
    here = lax.axis_index("row")
    per, rows, width = projections.shape
    nproj = per * ang
    seam_cols = LEFT * LANES

    halo = jnp.where(here == 0, projections[:, rows - REACH :], projections[:, :REACH])
    half_turn = [(i, (i + ang // 2) % ang) for i in range(ang)]
    across = [(i, 1 - i) for i in range(row)]
    both = [(a * row + r, b * row + s) for a, b in half_turn for r, s in across]
    seam_halo = lax.ppermute(halo[:, :, :seam_cols], ("ang", "row"), both)
    seam = lax.ppermute(projections[:, :, :seam_cols], "ang", half_turn)
    halo = lax.ppermute(halo, "row", across)

    taps = smooth_taps / jnp.sum(smooth_taps, axis=1, keepdims=True)
    ints = jnp.concatenate([correlation, offset, here[None].astype(jnp.int32)])
    early = early_side(ints, taps, projections)
    sent = source_side(ints, taps, early, projections, halo, seam, seam_halo)
    got = lax.all_to_all(sent.reshape(rows, per * BLOCKS, LANES), "ang", split_axis=0, concat_axis=0, tiled=True)
    return sinogram_side(got.reshape(nproj * BLOCKS, LANES), taps)[None, None]


def solution(mesh):
    P = jax.sharding.PartitionSpec
    placed = (P("ang", "row", None), P("ang"), P("ang"), P())
    return jax.shard_map(
        local, mesh=mesh, in_specs=placed, out_specs=P("row", "ang", None, None), check_vma=False
    )
```

```python
import functools
import math

import jax
import jax.numpy as jnp
import numpy as np
from jax import lax
from jax.experimental import pallas as pl
from jax.experimental.pallas import tpu as pltpu

ANGLE_TAPS = 31
LANES = 128
OUTER = 64
BLOCKS = 36
LEFT = 4
REACH = 16
TAPS = 2 * REACH + 1
LENGTH = OUTER * LANES
MIN_OVERLAP_OFFSET = 127
TOGETHER = 2
f32, bf16 = jnp.float32, jnp.bfloat16


def halves(x):
    high = x.astype(bf16)
    return high, (x - high.astype(f32)).astype(bf16)


def thirds(x):
    high = x.astype(bf16)
    rest = x - high.astype(f32)
    middle = rest.astype(bf16)
    return high, middle, (rest - middle.astype(f32)).astype(bf16)


def mxu(a, b):
    return jnp.dot(a, b, preferred_element_type=f32)


def row_matrices(taps, rows, sources, place_of):
    target = lax.broadcasted_iota(jnp.int32, (rows, 3 * sources), 0)
    at = lax.broadcasted_iota(jnp.int32, (rows, 3 * sources), 1)
    third = at // sources
    tap_at = place_of(at - third * sources) - target + REACH
    matrix = jnp.zeros((rows, 3 * sources), f32)
    for t in range(TAPS):
        matrix = jnp.where(tap_at == t, taps[1, t], matrix)
    high, mid, low = (part.astype(f32) for part in thirds(matrix))
    one = jnp.where(third == 1, mid, high).astype(bf16)
    two = jnp.where(third == 0, low, jnp.where(third == 1, mid, high)).astype(bf16)
    return one, two


def row_filter(matrices, field):
    high, mid, low = thirds(field)
    one = jnp.concatenate([high, high, mid], axis=0)
    two = jnp.concatenate([high, mid, low], axis=0)
    return mxu(matrices[0], one) + mxu(matrices[1], two)


def block_of(refs, s, block):
    last = refs[0].shape[2] // LANES - 1
    at = jnp.clip(block, 0, last) * LANES
    if not isinstance(at, int):
        at = pl.multiple_of(at, LANES)
    parts = [ref[s, :, pl.ds(at, LANES)] for ref in refs]
    return parts[0] if len(parts) == 1 else jnp.concatenate(parts, axis=0)


class Shifted:
    def __init__(self, ints, s, refs):
        self.overlap, self.lead = ints[s], ints[2 + s]
        self.shift = self.overlap - self.lead
        self.skip = self.shift // LANES
        turn = self.shift - self.skip * LANES
        self.back = lax.rem(LANES - turn, LANES)
        self.lane = lax.broadcasted_iota(jnp.int32, (1, LANES), 1)
        self.keep = self.lane < LANES - turn
        self.s, self.refs = s, refs

    def turned(self, block):
        return pltpu.roll(block_of(self.refs, self.s, block + self.skip), self.back, 1)

    def column(self, b):
        return LANES * b + self.shift + self.lane

    def plain_pair(self, b, width):
        parts = [self.turned(b + j) for j in range(3)]
        logs = []
        for j in range(2):
            value = jnp.where(self.keep, parts[j], parts[j + 1])
            logs.append(-jnp.log(jnp.where(self.column(b + j) < width, value, 1.0)))
        return jnp.concatenate(logs, axis=1)


def early_kernel(ints, taps, own, out):
    rows, width = own.shape[1], own.shape[2]
    matrices = row_matrices(taps, rows, rows, lambda at: at)
    for s in range(2):
        moved = Shifted(ints, s, [own])

        def pair(i, carry, s=s, moved=moved):
            at = pl.ds(pl.multiple_of((i - 1) * 2 * LANES, 2 * LANES), 2 * LANES)
            out[s, :, at] = row_filter(matrices, moved.plain_pair(2 * i, width))
            return carry

        lax.fori_loop(1, width // LANES // 2, pair, 0, unroll=3)


def source_kernel(ints, taps, early, own, halo, seam, seam_halo, out):
    rows, halo_rows, width = own.shape[1], halo.shape[1], halo.shape[2]
    every = rows + halo_rows
    row_group = ints[4]
    lane = lax.broadcasted_iota(jnp.int32, (1, LANES), 1)

    def across(at):
        return jnp.where((at >= rows) & (row_group > 0), at - every, at)

    matrices = row_matrices(taps, rows, every, across)
    halo_matrices = row_matrices(taps, rows, halo_rows, lambda at: across(at + rows))

    for s in range(2):

        def store(b, value, s=s):
            for g in range(rows // 8):
                at = pl.ds(8 * g * 2 * BLOCKS + s * BLOCKS + LEFT + b, 8, stride=2 * BLOCKS)
                out[at, :] = value[8 * g : 8 * g + 8]

        moved = Shifted(ints, s, [own, halo.at[:, :, : own.shape[2]]])
        overlap, lead, shift = moved.overlap, moved.lead, moved.shift
        mirror = jnp.broadcast_to((lead - 1 - lane) & (LANES - 1), (every, LANES))
        flipped = [
            jnp.take_along_axis(block_of([seam, seam_halo], s, j), mirror, axis=1, mode="promise_in_bounds")
            for j in range(LEFT)
        ]

        def blended(b, first, second):
            weight = jnp.clip((moved.column(b).astype(f32) + 0.5) / overlap.astype(f32), 0.0, 1.0)
            mine = jnp.where(moved.keep, first, second)
            other = jnp.where(lane < lead, flipped[min(max(-b, 0), 3)], flipped[min(max(-b - 1, 0), 3)])
            return -jnp.log(weight * mine + (1.0 - weight) * other)

        for b in range(-LEFT, 2, 2):
            parts = [moved.turned(b + i) for i in range(3)]
            logs = [blended(b + i, parts[i], parts[i + 1]) for i in range(2)]
            value = row_filter(matrices, jnp.concatenate(logs, axis=1))
            store(b, value[:, :LANES])
            store(b + 1, value[:, LANES:])

        rest = Shifted(ints, s, [halo])

        def pair(i, carry, s=s, store=store, rest=rest):
            b = 2 * i
            at = pl.ds(pl.multiple_of((b - 2) * LANES, 2 * LANES), 2 * LANES)
            value = early[s, :, at] + row_filter(halo_matrices, rest.plain_pair(b, width))
            store(b, value[:, :LANES])
            value = value[:, LANES:]
            last = b + 2 == width // LANES
            value = jnp.where(last & (lane == LANES - 1), rest.shift.astype(f32), value)
            value = jnp.where(last & (lane == LANES - 2) & (rest.shift > 1), rest.lead.astype(f32), value)
            store(b + 1, value)
            return carry

        lax.fori_loop(1, width // LANES // 2, pair, 0, unroll=15)


def times(a, b):
    return (a[0] * b[0] - a[1] * b[1], a[0] * b[1] + a[1] * b[0])


def dft(x, sign):
    n = len(x)
    if n == 1:
        return x
    even, odd = dft(x[0::2], sign), dft(x[1::2], sign)
    root = math.sqrt(0.5)
    first, second = [], []
    for k in range(n // 2):
        re, im = odd[k]
        if 4 * k == n:
            re, im = -sign * im, sign * re
        elif 8 * k == n:
            re, im = root * (re - sign * im), root * (im + sign * re)
        elif 8 * k == 3 * n:
            re, im = root * (-re - sign * im), root * (-im + sign * re)
        first.append((even[k][0] + re, even[k][1] + im))
        second.append((even[k][0] - re, even[k][1] - im))
    return first + second


def small_twist(value, power, sign):
    if power % OUTER == 0:
        return value
    angle = sign * 2.0 * math.pi * (power % OUTER) / OUTER
    return times(value, (np.float32(math.cos(angle)), np.float32(math.sin(angle))))


def sinogram_kernel(
    x, table, weights, out_hbm, out, field, mid_re, mid_im, rows, end_rows, sent
):
    gain_re, gain_im, twist_re, twist_im, end_u, end_v, ramp, _ = (
        table.at[OUTER * (k // 2) : OUTER * (k // 2 + 1), LANES * (k % 2) : LANES * (k % 2 + 1)] for k in range(8)
    )
    box = weights.at[: 2 * OUTER]
    forward, backward = ([weights.at[(at + k) * 2 * LANES - LANES : (at + k + 1) * 2 * LANES - LANES] for k in range(2)] for at in (1, 3))
    end_w = weights.at[5 * 2 * LANES - LANES :]
    half = out.shape[0] // 2
    lane = lax.broadcasted_iota(jnp.int32, (8, LANES), 1)

    def place(g, carry):
        sides = []
        for side in range(2):
            start = (side * half + 8 * g) * BLOCKS
            blocks = [x[pl.ds(start + k, 8, stride=BLOCKS), :] for k in range(BLOCKS)]
            last = blocks[-1]
            shift = last[:, LANES - 1 :]
            lead = jnp.where(shift > 1.5, last[:, LANES - 2 : LANES - 1], float(MIN_OVERLAP_OFFSET))
            hidden = (lane == LANES - 1) | ((lane == LANES - 2) & (shift > 1.5))
            blocks[-1] = jnp.where(hidden, 0.0, last)
            sides.append((blocks, shift.astype(jnp.int32), lead.astype(jnp.int32)))
        for side in range(2):
            mine, _, lead = sides[side]
            theirs, their_shift, _ = sides[1 - side]
            at = pl.ds(pl.multiple_of(side * half + 8 * g, 8), 8)
            spot = LANES - 1 + lead - their_shift - lane
            index = spot & (LANES - 1)
            jump = (spot >> 7) + 4
            mirrored = {}
            for k in range(OUTER // 2):
                mirrored[k] = jnp.take_along_axis(theirs[LEFT + k], index, axis=1, mode="promise_in_bounds")
            mirrored[-1] = mirrored[0]
            mirrored[OUTER // 2] = jnp.zeros((8, LANES), f32)
            for step in (1, 2, 4):
                moved = (jump & step) != 0
                top = OUTER // 2
                mirrored = {
                    k: jnp.where(moved, mirrored[min(k + step, top)], mirrored[k]) for k in mirrored
                }
            for c in range(OUTER // 2 - LEFT + 1):
                value = mirrored[OUTER // 2 - 5 - c]
                if c == OUTER // 2 - LEFT:
                    value = jnp.where(lane >= lead, mine[0], value)
                field[c, at, :] = value
            for k in range(1, BLOCKS):
                field[OUTER // 2 - LEFT + k, at, :] = mine[k]
        return carry

    lax.fori_loop(0, half // 8, place, 0, unroll=2)

    def highpass(i, carry):
        both = jnp.concatenate([field[2 * i], field[2 * i + 1]], axis=1)
        high, low = halves(both)
        sums = mxu(box[...], jnp.concatenate([high, low], axis=0))
        both = both - sums * np.float32(1.0 / ANGLE_TAPS)
        field[2 * i] = both[:, :LANES]
        field[2 * i + 1] = both[:, LANES:]
        return carry

    lax.fori_loop(0, OUTER // 2, highpass, 0, unroll=8)

    edge = lax.broadcasted_iota(jnp.int32, (1, LANES), 1) < LANES // 2
    border = [jnp.where(edge, field[0, at : at + half], field[OUTER - 1, at : at + half]) for at in (0, half)]
    tail_of = [table[4 * OUTER :, LANES * k : LANES * (k + 1)] for k in range(2)]
    tails = jnp.dot(border[0], tail_of[0], precision=lax.Precision.HIGHEST, preferred_element_type=f32)
    tails += jnp.dot(border[1], tail_of[1], precision=lax.Precision.HIGHEST, preferred_element_type=f32)
    end_rows[:, :LANES] = tails
    end_rows[:, LANES:] = pltpu.roll(tails, 2 * REACH, 1)

    def outer_forward(low_at, high_at, mid_re, mid_im, rows):
        for b in range(8):
            got = dft([(field[8 * a + b, low_at, :], field[8 * a + b, high_at, :]) for a in range(8)], -1.0)
            for d in range(8):
                mid_re[8 * d + b], mid_im[8 * d + b] = small_twist(got[d], d * b, -1.0)
        for d in range(8):
            got = dft([(mid_re[8 * d + b], mid_im[8 * d + b]) for b in range(8)], -1.0)
            for e in range(8):
                k = d + 8 * e
                re, im = times(got[e], (twist_re[k : k + 1, :], twist_im[k : k + 1, :]))
                rows[k, :, :LANES] = re
                rows[k, :, LANES:] = im

    def inner(low_at, rows):
        for part in range(2):
            n = OUTER // 2
            span = slice(part * n, (part + 1) * n)
            high, low = halves(rows[span].reshape(n * 8, 2 * LANES))
            spectrum = mxu(high, forward[0][...]) + mxu(low, forward[0][...]) + mxu(high, forward[1][...])
            spectrum = spectrum.reshape(n, 8, 2 * LANES)
            here = end_rows[low_at, :]
            tail = here[None, :, :LANES] * end_u[span][:, None, :] + here[None, :, LANES:] * end_v[span][:, None, :]
            tail = tail.reshape(n * 8, LANES)
            t_high = tail.astype(bf16).astype(f32)
            front = lax.broadcasted_iota(jnp.int32, (1, LANES), 1) < LANES // 2
            t_one = jnp.where(front, t_high, tail - t_high).astype(bf16)
            t_two = jnp.where(front, t_high, 0.0).astype(bf16)
            wrapped = mxu(jnp.concatenate([t_one, t_two], axis=1), end_w[...]).reshape(n, 8, 2 * LANES)
            g_re, g_im, r = gain_re[span][:, None, :], gain_im[span][:, None, :], ramp[span][:, None, :]
            re, im = times((spectrum[..., :LANES], spectrum[..., LANES:]), (g_re, g_im))
            re = re - r * wrapped[..., :LANES]
            im = im - r * wrapped[..., LANES:]
            high, low = halves(jnp.concatenate([re, im], axis=2).reshape(n * 8, 2 * LANES))
            signal = mxu(high, backward[0][...]) + mxu(low, backward[0][...]) + mxu(high, backward[1][...])
            signal = signal.reshape(n, 8, 2 * LANES)
            re, im = times(
                (signal[..., :LANES], signal[..., LANES:]), (twist_re[span][:, None, :], -twist_im[span][:, None, :])
            )
            rows[span, :, :LANES] = re
            rows[span, :, LANES:] = im

    def outer_backward(low_at, high_at, mid_re, mid_im, rows):
        for d in range(8):
            got = dft([(rows[d + 8 * e, :, :LANES], rows[d + 8 * e, :, LANES:]) for e in range(8)], 1.0)
            for b in range(8):
                mid_re[8 * d + b], mid_im[8 * d + b] = small_twist(got[b], d * b, 1.0)
        for b in range(8):
            got = dft([(mid_re[8 * d + b], mid_im[8 * d + b]) for d in range(8)], 1.0)
            for a in range(8):
                c = 8 * a + b
                out[low_at, c * LANES : (c + 1) * LANES] = got[a][0]
                out[high_at, c * LANES : (c + 1) * LANES] = got[a][1]

    def copies(g):
        for side in range(2):
            at = pl.ds(pl.multiple_of(side * half + 8 * g, 8), 8)
            yield pltpu.make_async_copy(out.at[at], out_hbm.at[at], sent.at[side, g])

    def filtered(i, carry):
        spots = []
        for j in range(TOGETHER):
            g = TOGETHER * i + j
            low_at = pl.ds(pl.multiple_of(8 * g, 8), 8)
            high_at = pl.ds(pl.multiple_of(half + 8 * g, 8), 8)
            spots.append((low_at, high_at, mid_re.at[j], mid_im.at[j], rows.at[j]))
        for spot in spots:
            outer_forward(*spot)
        for spot in spots:
            inner(spot[0], spot[4])
        for j, spot in enumerate(spots):
            outer_backward(*spot)
            for copy in copies(TOGETHER * i + j):
                copy.start()
        return carry

    lax.fori_loop(0, half // 8 // TOGETHER, filtered, 0)
    for g in range(half // 8):
        for copy in copies(g):
            copy.wait()


@functools.lru_cache(maxsize=None)
def tables(nproj):
    k1 = np.arange(OUTER)[:, None]
    l = np.arange(LANES)[None, :]
    angle = 2.0 * np.pi * (k1 * l % LENGTH) / LENGTH
    table = dict(twist_re=np.cos(angle), twist_im=-np.sin(angle))
    inner = 2.0 * np.pi * (np.arange(LANES)[:, None] * l % LANES) / LANES
    cos, sin = np.cos(inner), np.sin(inner)
    forward = np.block([[cos, -sin], [sin, cos]])
    backward = np.block([[cos, sin], [-sin, cos]])

    def two(w):
        high = w.astype(np.float32).astype(jnp.bfloat16)
        low = (w - high.astype(np.float64)).astype(np.float32).astype(jnp.bfloat16)
        return high, low

    table["forward"] = np.stack(two(forward))
    table["backward"] = np.stack(two(backward))
    columns = np.concatenate([np.arange(REACH), LENGTH - REACH + np.arange(REACH)])
    some = columns % LANES
    end_w = np.concatenate([forward[some], forward[LANES + some]], axis=0)
    high, low = two(end_w)
    table["end_w"] = np.concatenate([high, high, low, np.zeros_like(low)], axis=0)
    theta = 2.0 * np.pi * (k1 * columns[None, :] % LENGTH) / LENGTH
    table["end_u"] = np.tile(np.cos(theta), (1, 4))
    table["end_v"] = np.tile(np.concatenate([np.sin(theta), -np.sin(theta)], axis=1), (1, 2))
    tap_at = np.full((LANES, 2, 4, 2 * REACH), -1, np.int32)
    for i in range(REACH):
        for group in range(4):
            for t in range(TAPS):
                if LANES - REACH + i + t < LANES:
                    tap_at[LANES - REACH + i + t, group % 2, group, i] = t
                if i + t - 2 * REACH >= 0:
                    tap_at[i + t - 2 * REACH, group % 2, group, REACH + i] = t
    table["tap_at"] = tap_at.reshape(LANES, 2 * LANES)
    frequency = k1 + OUTER * l
    table["ramp"] = np.minimum(frequency, LENGTH - frequency) / (LENGTH / 2) / LENGTH
    lag = np.arange(TAPS) - REACH
    a = 2.0 * np.pi * (k1 * lag[None, :] % LENGTH) / LENGTH
    b = 2.0 * np.pi * (lag[:, None] * l % LANES) / LANES
    table["gain_left"] = np.stack(
        [np.concatenate([np.cos(a), -np.sin(a)], axis=1), np.concatenate([np.sin(a), np.cos(a)], axis=1)]
    )
    table["gain_right"] = np.concatenate([np.cos(b), np.sin(b)], axis=0)
    p = np.arange(nproj)
    gap = (p[:, None] - p[None, :]) % nproj
    near = (np.minimum(gap, nproj - gap) <= ANGLE_TAPS // 2).astype(np.float32).astype(jnp.bfloat16)
    table["box"] = np.concatenate([near, near], axis=1)
    pairs = (("twist_re", "twist_im"), ("end_u", "end_v"), ("ramp", "ramp"))
    fixed = np.block([[table[k] for k in pair] for pair in pairs]).astype(np.float32)
    weights = np.concatenate([table["box"], *table["forward"], *table["backward"], table["end_w"]], axis=0)
    gain = [table[k].astype(np.float32) for k in ("gain_left", "gain_right")]
    return fixed, weights, gain, table["tap_at"]


def vmem_spec():
    return pl.BlockSpec(memory_space=pltpu.VMEM)


def hbm_spec():
    return pl.BlockSpec(memory_space=pl.ANY)


def smem_spec():
    return pl.BlockSpec(memory_space=pltpu.SMEM)


def early_side(ints, taps, projections):
    per, rows, width = projections.shape
    shape = jax.ShapeDtypeStruct((per, rows, width - 2 * LANES), f32)
    return pl.pallas_call(
        early_kernel,
        out_shape=shape,
        in_specs=[smem_spec(), smem_spec(), vmem_spec()],
        out_specs=vmem_spec(),
        compiler_params=pltpu.CompilerParams(vmem_limit_bytes=24 * 1024 * 1024),
        cost_estimate=pl.CostEstimate(flops=12 * per * rows * rows * width, bytes_accessed=8 * per * rows * width, transcendentals=per * rows * width),
        name="early",
    )(ints, taps, projections)


def source_side(ints, taps, early, projections, halo, seam, seam_halo):
    per, rows, _ = projections.shape
    return pl.pallas_call(
        source_kernel,
        grid=(1,),
        out_shape=jax.ShapeDtypeStruct((rows * per * BLOCKS, LANES), f32),
        in_specs=[smem_spec(), smem_spec(), vmem_spec(), pl.BlockSpec((per, rows, 8 * LANES), lambda i: (0, 0, 0))]
        + [vmem_spec()] * 3,
        out_specs=vmem_spec(),
        compiler_params=pltpu.CompilerParams(vmem_limit_bytes=24 * 1024 * 1024),
        name="source",
    )(ints, taps, early, projections, halo, seam, seam_halo)


def sinogram_side(got, taps):
    nproj = got.shape[0] // BLOCKS
    fixed, weights, (gain_left, gain_right), tap_at = tables(nproj)
    left = (gain_left * jnp.tile(taps[0], 2)).reshape(2 * OUTER, 2 * TAPS)
    gain = jnp.dot(left, gain_right, precision=lax.Precision.HIGHEST) * jnp.tile(fixed[2 * OUTER :, :LANES], (2, 1))
    ends = jnp.zeros(tap_at.shape, f32)
    for k in range(TAPS):
        ends = jnp.where(tap_at == k, taps[0, k], ends)
    table = jnp.concatenate([jnp.concatenate([gain[:OUTER], gain[OUTER:]], axis=1), fixed, ends], axis=0)
    return pl.pallas_call(
        sinogram_kernel,
        out_shape=jax.ShapeDtypeStruct((nproj, LENGTH), f32),
        in_specs=[vmem_spec()] * 3,
        out_specs=hbm_spec(),
        scratch_shapes=[
            pltpu.VMEM((nproj, LENGTH), f32),
            pltpu.VMEM((OUTER, nproj, LANES), f32),
            pltpu.VMEM((TOGETHER, OUTER, 8, LANES), f32),
            pltpu.VMEM((TOGETHER, OUTER, 8, LANES), f32),
            pltpu.VMEM((TOGETHER, OUTER, 8, 2 * LANES), f32),
            pltpu.VMEM((nproj // 2, 2 * LANES), f32),
            pltpu.SemaphoreType.DMA((2, nproj // 16)),
        ],
        compiler_params=pltpu.CompilerParams(vmem_limit_bytes=28 * 1024 * 1024),
        name="sinogram",
    )(got, table, jnp.asarray(weights))


def local(projections, correlation, offset, smooth_taps):
    ang, row = lax.axis_size("ang"), lax.axis_size("row")
    here = lax.axis_index("row")
    per, rows, width = projections.shape
    nproj = per * ang
    seam_cols = LEFT * LANES

    halo = jnp.where(here == 0, projections[:, rows - REACH :], projections[:, :REACH])
    half_turn = [(i, (i + ang // 2) % ang) for i in range(ang)]
    across = [(i, 1 - i) for i in range(row)]
    both = [(a * row + r, b * row + s) for a, b in half_turn for r, s in across]
    seam_halo = lax.ppermute(halo[:, :, :seam_cols], ("ang", "row"), both)
    seam = lax.ppermute(projections[:, :, :seam_cols], "ang", half_turn)
    halo = lax.ppermute(halo, "row", across)

    taps = smooth_taps / jnp.sum(smooth_taps, axis=1, keepdims=True)
    ints = jnp.concatenate([correlation, offset, here[None].astype(jnp.int32)])
    early = early_side(ints, taps, projections)
    sent = source_side(ints, taps, early, projections, halo, seam, seam_halo)
    got = lax.all_to_all(sent.reshape(rows, per * BLOCKS, LANES), "ang", split_axis=0, concat_axis=0, tiled=True)
    return sinogram_side(got.reshape(nproj * BLOCKS, LANES), taps)[None, None]


def solution(mesh):
    P = jax.sharding.PartitionSpec
    placed = (P("ang", "row", None), P("ang"), P("ang"), P())
    return jax.shard_map(
        local, mesh=mesh, in_specs=placed, out_specs=P("row", "ang", None, None), check_vma=False
    )
```

```python
import functools
import math

import jax
import jax.numpy as jnp
import numpy as np
from jax import lax
from jax.experimental import pallas as pl
from jax.experimental.pallas import tpu as pltpu

ANGLE_TAPS = 31
LANES = 128
OUTER = 64
BLOCKS = 36
LEFT = 4
REACH = 16
TAPS = 2 * REACH + 1
LENGTH = OUTER * LANES
MIN_OVERLAP_OFFSET = 127
TOGETHER = 2
f32, bf16 = jnp.float32, jnp.bfloat16


def halves(x):
    high = x.astype(bf16)
    return high, (x - high.astype(f32)).astype(bf16)


def thirds(x):
    high = x.astype(bf16)
    rest = x - high.astype(f32)
    middle = rest.astype(bf16)
    return high, middle, (rest - middle.astype(f32)).astype(bf16)


def mxu(a, b):
    return jnp.dot(a, b, preferred_element_type=f32)


def row_matrices(taps, rows, sources, place_of):
    target = lax.broadcasted_iota(jnp.int32, (rows, 3 * sources), 0)
    at = lax.broadcasted_iota(jnp.int32, (rows, 3 * sources), 1)
    third = at // sources
    tap_at = place_of(at - third * sources) - target + REACH
    matrix = jnp.zeros((rows, 3 * sources), f32)
    for t in range(TAPS):
        matrix = jnp.where(tap_at == t, taps[1, t], matrix)
    high, mid, low = (part.astype(f32) for part in thirds(matrix))
    one = jnp.where(third == 1, mid, high).astype(bf16)
    two = jnp.where(third == 0, low, jnp.where(third == 1, mid, high)).astype(bf16)
    return one, two


def row_filter(matrices, field):
    high, mid, low = thirds(field)
    one = jnp.concatenate([high, high, mid], axis=0)
    two = jnp.concatenate([high, mid, low], axis=0)
    return mxu(matrices[0], one) + mxu(matrices[1], two)


def block_of(refs, s, block):
    last = refs[0].shape[2] // LANES - 1
    at = jnp.clip(block, 0, last) * LANES
    if not isinstance(at, int):
        at = pl.multiple_of(at, LANES)
    parts = [ref[s, :, pl.ds(at, LANES)] for ref in refs]
    return parts[0] if len(parts) == 1 else jnp.concatenate(parts, axis=0)


class Shifted:
    def __init__(self, ints, s, refs):
        self.overlap, self.lead = ints[s], ints[2 + s]
        self.shift = self.overlap - self.lead
        self.skip = self.shift // LANES
        turn = self.shift - self.skip * LANES
        self.back = lax.rem(LANES - turn, LANES)
        self.lane = lax.broadcasted_iota(jnp.int32, (1, LANES), 1)
        self.keep = self.lane < LANES - turn
        self.s, self.refs = s, refs

    def turned(self, block):
        return pltpu.roll(block_of(self.refs, self.s, block + self.skip), self.back, 1)

    def column(self, b):
        return LANES * b + self.shift + self.lane

    def plain_pair(self, b, width):
        parts = [self.turned(b + j) for j in range(3)]
        logs = []
        for j in range(2):
            value = jnp.where(self.keep, parts[j], parts[j + 1])
            logs.append(-jnp.log(jnp.where(self.column(b + j) < width, value, 1.0)))
        return jnp.concatenate(logs, axis=1)


def early_kernel(ints, taps, own, out):
    rows, width = own.shape[1], own.shape[2]
    matrices = row_matrices(taps, rows, rows, lambda at: at)
    for s in range(2):
        moved = Shifted(ints, s, [own])

        def pair(i, carry, s=s, moved=moved):
            at = pl.ds(pl.multiple_of((i - 1) * 2 * LANES, 2 * LANES), 2 * LANES)
            out[s, :, at] = row_filter(matrices, moved.plain_pair(2 * i, width))
            return carry

        lax.fori_loop(1, width // LANES // 2, pair, 0, unroll=3)


def source_kernel(ints, taps, early, own, halo, seam, seam_halo, out):
    rows, halo_rows, width = own.shape[1], halo.shape[1], halo.shape[2]
    every = rows + halo_rows
    row_group = ints[4]
    lane = lax.broadcasted_iota(jnp.int32, (1, LANES), 1)

    def across(at):
        return jnp.where((at >= rows) & (row_group > 0), at - every, at)

    matrices = row_matrices(taps, rows, every, across)
    halo_matrices = row_matrices(taps, rows, halo_rows, lambda at: across(at + rows))

    for s in range(2):

        def store(b, value, s=s):
            for g in range(rows // 8):
                at = pl.ds(8 * g * 2 * BLOCKS + s * BLOCKS + LEFT + b, 8, stride=2 * BLOCKS)
                out[at, :] = value[8 * g : 8 * g + 8]

        moved = Shifted(ints, s, [own, halo.at[:, :, : own.shape[2]]])
        overlap, lead, shift = moved.overlap, moved.lead, moved.shift
        mirror = jnp.broadcast_to((lead - 1 - lane) & (LANES - 1), (every, LANES))
        flipped = [
            jnp.take_along_axis(block_of([seam, seam_halo], s, j), mirror, axis=1, mode="promise_in_bounds")
            for j in range(LEFT)
        ]

        def blended(b, first, second):
            weight = jnp.clip((moved.column(b).astype(f32) + 0.5) / overlap.astype(f32), 0.0, 1.0)
            mine = jnp.where(moved.keep, first, second)
            other = jnp.where(lane < lead, flipped[min(max(-b, 0), 3)], flipped[min(max(-b - 1, 0), 3)])
            return -jnp.log(weight * mine + (1.0 - weight) * other)

        for b in range(-LEFT, 2, 2):
            parts = [moved.turned(b + i) for i in range(3)]
            logs = [blended(b + i, parts[i], parts[i + 1]) for i in range(2)]
            value = row_filter(matrices, jnp.concatenate(logs, axis=1))
            store(b, value[:, :LANES])
            store(b + 1, value[:, LANES:])

        rest = Shifted(ints, s, [halo])

        def pair(i, carry, s=s, store=store, rest=rest):
            b = 2 * i
            at = pl.ds(pl.multiple_of((b - 2) * LANES, 2 * LANES), 2 * LANES)
            value = early[s, :, at] + row_filter(halo_matrices, rest.plain_pair(b, width))
            store(b, value[:, :LANES])
            value = value[:, LANES:]
            last = b + 2 == width // LANES
            value = jnp.where(last & (lane == LANES - 1), rest.shift.astype(f32), value)
            value = jnp.where(last & (lane == LANES - 2) & (rest.shift > 1), rest.lead.astype(f32), value)
            store(b + 1, value)
            return carry

        lax.fori_loop(1, width // LANES // 2, pair, 0, unroll=15)


def times(a, b):
    return (a[0] * b[0] - a[1] * b[1], a[0] * b[1] + a[1] * b[0])


def dft(x, sign):
    n = len(x)
    if n == 1:
        return x
    even, odd = dft(x[0::2], sign), dft(x[1::2], sign)
    root = math.sqrt(0.5)
    first, second = [], []
    for k in range(n // 2):
        re, im = odd[k]
        if 4 * k == n:
            re, im = -sign * im, sign * re
        elif 8 * k == n:
            re, im = root * (re - sign * im), root * (im + sign * re)
        elif 8 * k == 3 * n:
            re, im = root * (-re - sign * im), root * (-im + sign * re)
        first.append((even[k][0] + re, even[k][1] + im))
        second.append((even[k][0] - re, even[k][1] - im))
    return first + second


def small_twist(value, power, sign):
    if power % OUTER == 0:
        return value
    angle = sign * 2.0 * math.pi * (power % OUTER) / OUTER
    return times(value, (np.float32(math.cos(angle)), np.float32(math.sin(angle))))


def sinogram_kernel(
    x, table, weights, out_hbm, out, field, mid_re, mid_im, rows, end_rows, sent
):
    gain_re, gain_im, twist_re, twist_im, end_u, end_v, ramp, _ = (
        table.at[OUTER * (k // 2) : OUTER * (k // 2 + 1), LANES * (k % 2) : LANES * (k % 2 + 1)] for k in range(8)
    )
    box = weights.at[: 2 * OUTER]
    forward, backward = ([weights.at[(at + k) * 2 * LANES - LANES : (at + k + 1) * 2 * LANES - LANES] for k in range(2)] for at in (1, 3))
    end_w = weights.at[5 * 2 * LANES - LANES :]
    half = out.shape[0] // 2
    lane = lax.broadcasted_iota(jnp.int32, (8, LANES), 1)

    def place(g, carry):
        sides = []
        for side in range(2):
            start = (side * half + 8 * g) * BLOCKS
            blocks = [x[pl.ds(start + k, 8, stride=BLOCKS), :] for k in range(BLOCKS)]
            last = blocks[-1]
            shift = last[:, LANES - 1 :]
            lead = jnp.where(shift > 1.5, last[:, LANES - 2 : LANES - 1], float(MIN_OVERLAP_OFFSET))
            hidden = (lane == LANES - 1) | ((lane == LANES - 2) & (shift > 1.5))
            blocks[-1] = jnp.where(hidden, 0.0, last)
            sides.append((blocks, shift.astype(jnp.int32), lead.astype(jnp.int32)))
        for side in range(2):
            mine, _, lead = sides[side]
            theirs, their_shift, _ = sides[1 - side]
            at = pl.ds(pl.multiple_of(side * half + 8 * g, 8), 8)
            spot = LANES - 1 + lead - their_shift - lane
            index = spot & (LANES - 1)
            jump = (spot >> 7) + 4
            mirrored = {}
            for k in range(OUTER // 2):
                mirrored[k] = jnp.take_along_axis(theirs[LEFT + k], index, axis=1, mode="promise_in_bounds")
            mirrored[-1] = mirrored[0]
            mirrored[OUTER // 2] = jnp.zeros((8, LANES), f32)
            for step in (1, 2, 4):
                moved = (jump & step) != 0
                top = OUTER // 2
                mirrored = {
                    k: jnp.where(moved, mirrored[min(k + step, top)], mirrored[k]) for k in mirrored
                }
            for c in range(OUTER // 2 - LEFT + 1):
                value = mirrored[OUTER // 2 - 5 - c]
                if c == OUTER // 2 - LEFT:
                    value = jnp.where(lane >= lead, mine[0], value)
                field[c, at, :] = value
            for k in range(1, BLOCKS):
                field[OUTER // 2 - LEFT + k, at, :] = mine[k]
        return carry

    lax.fori_loop(0, half // 8, place, 0, unroll=2)

    def highpass(i, carry):
        both = jnp.concatenate([field[2 * i], field[2 * i + 1]], axis=1)
        high, low = halves(both)
        sums = mxu(box[...], jnp.concatenate([high, low], axis=0))
        both = both - sums * np.float32(1.0 / ANGLE_TAPS)
        field[2 * i] = both[:, :LANES]
        field[2 * i + 1] = both[:, LANES:]
        return carry

    lax.fori_loop(0, OUTER // 2, highpass, 0, unroll=8)

    edge = lax.broadcasted_iota(jnp.int32, (1, LANES), 1) < LANES // 2
    border = [jnp.where(edge, field[0, at : at + half], field[OUTER - 1, at : at + half]) for at in (0, half)]
    tail_of = [table[4 * OUTER :, LANES * k : LANES * (k + 1)] for k in range(2)]
    tails = jnp.dot(border[0], tail_of[0], precision=lax.Precision.HIGHEST, preferred_element_type=f32)
    tails += jnp.dot(border[1], tail_of[1], precision=lax.Precision.HIGHEST, preferred_element_type=f32)
    end_rows[:, :LANES] = tails
    end_rows[:, LANES:] = pltpu.roll(tails, 2 * REACH, 1)

    def outer_forward(low_at, high_at, mid_re, mid_im, rows):
        for b in range(8):
            got = dft([(field[8 * a + b, low_at, :], field[8 * a + b, high_at, :]) for a in range(8)], -1.0)
            for d in range(8):
                mid_re[8 * d + b], mid_im[8 * d + b] = small_twist(got[d], d * b, -1.0)
        for d in range(8):
            got = dft([(mid_re[8 * d + b], mid_im[8 * d + b]) for b in range(8)], -1.0)
            for e in range(8):
                k = d + 8 * e
                re, im = times(got[e], (twist_re[k : k + 1, :], twist_im[k : k + 1, :]))
                rows[k, :, :LANES] = re
                rows[k, :, LANES:] = im

    def inner(low_at, rows):
        for part in range(2):
            n = OUTER // 2
            span = slice(part * n, (part + 1) * n)
            high, low = halves(rows[span].reshape(n * 8, 2 * LANES))
            spectrum = mxu(high, forward[0][...]) + mxu(low, forward[0][...]) + mxu(high, forward[1][...])
            spectrum = spectrum.reshape(n, 8, 2 * LANES)
            here = end_rows[low_at, :]
            tail = here[None, :, :LANES] * end_u[span][:, None, :] + here[None, :, LANES:] * end_v[span][:, None, :]
            tail = tail.reshape(n * 8, LANES)
            t_high = tail.astype(bf16).astype(f32)
            front = lax.broadcasted_iota(jnp.int32, (1, LANES), 1) < LANES // 2
            t_one = jnp.where(front, t_high, tail - t_high).astype(bf16)
            wrapped = mxu(jnp.concatenate([t_one, t_one], axis=1), end_w[...]).reshape(n, 8, 2 * LANES)
            g_re, g_im, r = gain_re[span][:, None, :], gain_im[span][:, None, :], ramp[span][:, None, :]
            re, im = times((spectrum[..., :LANES], spectrum[..., LANES:]), (g_re, g_im))
            re = re - r * wrapped[..., :LANES]
            im = im - r * wrapped[..., LANES:]
            high, low = halves(jnp.concatenate([re, im], axis=2).reshape(n * 8, 2 * LANES))
            signal = mxu(high, backward[0][...]) + mxu(low, backward[0][...]) + mxu(high, backward[1][...])
            signal = signal.reshape(n, 8, 2 * LANES)
            re, im = times(
                (signal[..., :LANES], signal[..., LANES:]), (twist_re[span][:, None, :], -twist_im[span][:, None, :])
            )
            rows[span, :, :LANES] = re
            rows[span, :, LANES:] = im

    def outer_backward(low_at, high_at, mid_re, mid_im, rows):
        for d in range(8):
            got = dft([(rows[d + 8 * e, :, :LANES], rows[d + 8 * e, :, LANES:]) for e in range(8)], 1.0)
            for b in range(8):
                mid_re[8 * d + b], mid_im[8 * d + b] = small_twist(got[b], d * b, 1.0)
        for b in range(8):
            got = dft([(mid_re[8 * d + b], mid_im[8 * d + b]) for d in range(8)], 1.0)
            for a in range(8):
                c = 8 * a + b
                out[low_at, c * LANES : (c + 1) * LANES] = got[a][0]
                out[high_at, c * LANES : (c + 1) * LANES] = got[a][1]

    def copies(g):
        for side in range(2):
            at = pl.ds(pl.multiple_of(side * half + 8 * g, 8), 8)
            yield pltpu.make_async_copy(out.at[at], out_hbm.at[at], sent.at[side, g])

    def filtered(i, carry):
        spots = []
        for j in range(TOGETHER):
            g = TOGETHER * i + j
            low_at = pl.ds(pl.multiple_of(8 * g, 8), 8)
            high_at = pl.ds(pl.multiple_of(half + 8 * g, 8), 8)
            spots.append((low_at, high_at, mid_re.at[j], mid_im.at[j], rows.at[j]))
        for spot in spots:
            outer_forward(*spot)
        for spot in spots:
            inner(spot[0], spot[4])
        for j, spot in enumerate(spots):
            outer_backward(*spot)
            for copy in copies(TOGETHER * i + j):
                copy.start()
        return carry

    lax.fori_loop(0, half // 8 // TOGETHER, filtered, 0)
    for g in range(half // 8):
        for copy in copies(g):
            copy.wait()


@functools.lru_cache(maxsize=None)
def tables(nproj):
    k1 = np.arange(OUTER)[:, None]
    l = np.arange(LANES)[None, :]
    angle = 2.0 * np.pi * (k1 * l % LENGTH) / LENGTH
    table = dict(twist_re=np.cos(angle), twist_im=-np.sin(angle))
    inner = 2.0 * np.pi * (np.arange(LANES)[:, None] * l % LANES) / LANES
    cos, sin = np.cos(inner), np.sin(inner)
    forward = np.block([[cos, -sin], [sin, cos]])
    backward = np.block([[cos, sin], [-sin, cos]])

    def two(w):
        high = w.astype(np.float32).astype(jnp.bfloat16)
        low = (w - high.astype(np.float64)).astype(np.float32).astype(jnp.bfloat16)
        return high, low

    table["forward"] = np.stack(two(forward))
    table["backward"] = np.stack(two(backward))
    columns = np.concatenate([np.arange(REACH), LENGTH - REACH + np.arange(REACH)])
    some = columns % LANES
    end_w = np.concatenate([forward[some], forward[LANES + some]], axis=0)
    high, low = two(end_w)
    table["end_w"] = np.concatenate([high, high, low, np.zeros_like(low)], axis=0)
    theta = 2.0 * np.pi * (k1 * columns[None, :] % LENGTH) / LENGTH
    table["end_u"] = np.tile(np.cos(theta), (1, 4))
    table["end_v"] = np.tile(np.concatenate([np.sin(theta), -np.sin(theta)], axis=1), (1, 2))
    tap_at = np.full((LANES, 2, 4, 2 * REACH), -1, np.int32)
    for i in range(REACH):
        for group in range(4):
            for t in range(TAPS):
                if LANES - REACH + i + t < LANES:
                    tap_at[LANES - REACH + i + t, group % 2, group, i] = t
                if i + t - 2 * REACH >= 0:
                    tap_at[i + t - 2 * REACH, group % 2, group, REACH + i] = t
    table["tap_at"] = tap_at.reshape(LANES, 2 * LANES)
    frequency = k1 + OUTER * l
    table["ramp"] = np.minimum(frequency, LENGTH - frequency) / (LENGTH / 2) / LENGTH
    lag = np.arange(TAPS) - REACH
    a = 2.0 * np.pi * (k1 * lag[None, :] % LENGTH) / LENGTH
    b = 2.0 * np.pi * (lag[:, None] * l % LANES) / LANES
    table["gain_left"] = np.stack(
        [np.concatenate([np.cos(a), -np.sin(a)], axis=1), np.concatenate([np.sin(a), np.cos(a)], axis=1)]
    )
    table["gain_right"] = np.concatenate([np.cos(b), np.sin(b)], axis=0)
    p = np.arange(nproj)
    gap = (p[:, None] - p[None, :]) % nproj
    near = (np.minimum(gap, nproj - gap) <= ANGLE_TAPS // 2).astype(np.float32).astype(jnp.bfloat16)
    table["box"] = np.concatenate([near, near], axis=1)
    pairs = (("twist_re", "twist_im"), ("end_u", "end_v"), ("ramp", "ramp"))
    fixed = np.block([[table[k] for k in pair] for pair in pairs]).astype(np.float32)
    weights = np.concatenate([table["box"], *table["forward"], *table["backward"], table["end_w"]], axis=0)
    gain = [table[k].astype(np.float32) for k in ("gain_left", "gain_right")]
    return fixed, weights, gain, table["tap_at"]


def vmem_spec():
    return pl.BlockSpec(memory_space=pltpu.VMEM)


def hbm_spec():
    return pl.BlockSpec(memory_space=pl.ANY)


def smem_spec():
    return pl.BlockSpec(memory_space=pltpu.SMEM)


def early_side(ints, taps, projections):
    per, rows, width = projections.shape
    shape = jax.ShapeDtypeStruct((per, rows, width - 2 * LANES), f32)
    return pl.pallas_call(
        early_kernel,
        out_shape=shape,
        in_specs=[smem_spec(), smem_spec(), vmem_spec()],
        out_specs=vmem_spec(),
        compiler_params=pltpu.CompilerParams(vmem_limit_bytes=24 * 1024 * 1024),
        cost_estimate=pl.CostEstimate(flops=12 * per * rows * rows * width, bytes_accessed=8 * per * rows * width, transcendentals=per * rows * width),
        name="early",
    )(ints, taps, projections)


def source_side(ints, taps, early, projections, halo, seam, seam_halo):
    per, rows, _ = projections.shape
    return pl.pallas_call(
        source_kernel,
        grid=(1,),
        out_shape=jax.ShapeDtypeStruct((rows * per * BLOCKS, LANES), f32),
        in_specs=[smem_spec(), smem_spec(), vmem_spec(), pl.BlockSpec((per, rows, 8 * LANES), lambda i: (0, 0, 0))]
        + [vmem_spec()] * 3,
        out_specs=vmem_spec(),
        compiler_params=pltpu.CompilerParams(vmem_limit_bytes=24 * 1024 * 1024),
        name="source",
    )(ints, taps, early, projections, halo, seam, seam_halo)


def sinogram_side(got, taps):
    nproj = got.shape[0] // BLOCKS
    fixed, weights, (gain_left, gain_right), tap_at = tables(nproj)
    left = (gain_left * jnp.tile(taps[0], 2)).reshape(2 * OUTER, 2 * TAPS)
    gain = jnp.dot(left, gain_right, precision=lax.Precision.HIGHEST) * jnp.tile(fixed[2 * OUTER :, :LANES], (2, 1))
    ends = jnp.zeros(tap_at.shape, f32)
    for k in range(TAPS):
        ends = jnp.where(tap_at == k, taps[0, k], ends)
    table = jnp.concatenate([jnp.concatenate([gain[:OUTER], gain[OUTER:]], axis=1), fixed, ends], axis=0)
    return pl.pallas_call(
        sinogram_kernel,
        out_shape=jax.ShapeDtypeStruct((nproj, LENGTH), f32),
        in_specs=[vmem_spec()] * 3,
        out_specs=hbm_spec(),
        scratch_shapes=[
            pltpu.VMEM((nproj, LENGTH), f32),
            pltpu.VMEM((OUTER, nproj, LANES), f32),
            pltpu.VMEM((TOGETHER, OUTER, 8, LANES), f32),
            pltpu.VMEM((TOGETHER, OUTER, 8, LANES), f32),
            pltpu.VMEM((TOGETHER, OUTER, 8, 2 * LANES), f32),
            pltpu.VMEM((nproj // 2, 2 * LANES), f32),
            pltpu.SemaphoreType.DMA((2, nproj // 16)),
        ],
        compiler_params=pltpu.CompilerParams(vmem_limit_bytes=28 * 1024 * 1024),
        name="sinogram",
    )(got, table, jnp.asarray(weights))


def local(projections, correlation, offset, smooth_taps):
    ang, row = lax.axis_size("ang"), lax.axis_size("row")
    here = lax.axis_index("row")
    per, rows, width = projections.shape
    nproj = per * ang
    seam_cols = LEFT * LANES

    halo = jnp.where(here == 0, projections[:, rows - REACH :], projections[:, :REACH])
    half_turn = [(i, (i + ang // 2) % ang) for i in range(ang)]
    across = [(i, 1 - i) for i in range(row)]
    both = [(a * row + r, b * row + s) for a, b in half_turn for r, s in across]
    seam_halo = lax.ppermute(halo[:, :, :seam_cols], ("ang", "row"), both)
    seam = lax.ppermute(projections[:, :, :seam_cols], "ang", half_turn)
    halo = lax.ppermute(halo, "row", across)

    taps = smooth_taps / jnp.sum(smooth_taps, axis=1, keepdims=True)
    ints = jnp.concatenate([correlation, offset, here[None].astype(jnp.int32)])
    early = early_side(ints, taps, projections)
    sent = source_side(ints, taps, early, projections, halo, seam, seam_halo)
    got = lax.all_to_all(sent.reshape(rows, per * BLOCKS, LANES), "ang", split_axis=0, concat_axis=0, tiled=True)
    return sinogram_side(got.reshape(nproj * BLOCKS, LANES), taps)[None, None]


def solution(mesh):
    P = jax.sharding.PartitionSpec
    placed = (P("ang", "row", None), P("ang"), P("ang"), P())
    return jax.shard_map(
        local, mesh=mesh, in_specs=placed, out_specs=P("row", "ang", None, None), check_vma=False
    )
```

```python
import functools
import math

import jax
import jax.numpy as jnp
import numpy as np
from jax import lax
from jax.experimental import pallas as pl
from jax.experimental.pallas import tpu as pltpu

ANGLE_TAPS = 31
LANES = 128
OUTER = 64
BLOCKS = 36
LEFT = 4
REACH = 16
TAPS = 2 * REACH + 1
LENGTH = OUTER * LANES
MIN_OVERLAP_OFFSET = 127
TOGETHER = 2
f32, bf16 = jnp.float32, jnp.bfloat16


def halves(x):
    high = x.astype(bf16)
    return high, (x - high.astype(f32)).astype(bf16)


def thirds(x):
    high = x.astype(bf16)
    rest = x - high.astype(f32)
    middle = rest.astype(bf16)
    return high, middle, (rest - middle.astype(f32)).astype(bf16)


def mxu(a, b):
    return jnp.dot(a, b, preferred_element_type=f32)


def row_matrices(taps, rows, sources, place_of):
    target = lax.broadcasted_iota(jnp.int32, (rows, 3 * sources), 0)
    at = lax.broadcasted_iota(jnp.int32, (rows, 3 * sources), 1)
    third = at // sources
    tap_at = place_of(at - third * sources) - target + REACH
    matrix = jnp.zeros((rows, 3 * sources), f32)
    for t in range(TAPS):
        matrix = jnp.where(tap_at == t, taps[1, t], matrix)
    high, mid, low = (part.astype(f32) for part in thirds(matrix))
    one = jnp.where(third == 1, mid, high).astype(bf16)
    two = jnp.where(third == 0, low, jnp.where(third == 1, mid, high)).astype(bf16)
    return one, two


def row_filter(matrices, field):
    high, mid, low = thirds(field)
    one = jnp.concatenate([high, high, mid], axis=0)
    two = jnp.concatenate([high, mid, low], axis=0)
    return mxu(matrices[0], one) + mxu(matrices[1], two)


def block_of(refs, s, block):
    last = refs[0].shape[2] // LANES - 1
    at = jnp.clip(block, 0, last) * LANES
    if not isinstance(at, int):
        at = pl.multiple_of(at, LANES)
    parts = [ref[s, :, pl.ds(at, LANES)] for ref in refs]
    return parts[0] if len(parts) == 1 else jnp.concatenate(parts, axis=0)


class Shifted:
    def __init__(self, ints, s, refs):
        self.overlap, self.lead = ints[s], ints[2 + s]
        self.shift = self.overlap - self.lead
        self.skip = self.shift // LANES
        turn = self.shift - self.skip * LANES
        self.back = lax.rem(LANES - turn, LANES)
        self.lane = lax.broadcasted_iota(jnp.int32, (1, LANES), 1)
        self.keep = self.lane < LANES - turn
        self.s, self.refs = s, refs

    def turned(self, block):
        return pltpu.roll(block_of(self.refs, self.s, block + self.skip), self.back, 1)

    def column(self, b):
        return LANES * b + self.shift + self.lane

    def plain_pair(self, b, width):
        parts = [self.turned(b + j) for j in range(3)]
        logs = []
        for j in range(2):
            value = jnp.where(self.keep, parts[j], parts[j + 1])
            logs.append(-jnp.log(jnp.where(self.column(b + j) < width, value, 1.0)))
        return jnp.concatenate(logs, axis=1)


def early_kernel(ints, taps, own, out):
    rows, width = own.shape[1], own.shape[2]
    matrices = row_matrices(taps, rows, rows, lambda at: at)
    for s in range(2):
        moved = Shifted(ints, s, [own])

        def pair(i, carry, s=s, moved=moved):
            at = pl.ds(pl.multiple_of((i - 1) * 2 * LANES, 2 * LANES), 2 * LANES)
            out[s, :, at] = row_filter(matrices, moved.plain_pair(2 * i, width))
            return carry

        lax.fori_loop(1, width // LANES // 2, pair, 0, unroll=3)


def source_kernel(ints, taps, early, own, halo, seam, seam_halo, out):
    rows, halo_rows, width = own.shape[1], halo.shape[1], halo.shape[2]
    every = rows + halo_rows
    row_group = ints[4]
    lane = lax.broadcasted_iota(jnp.int32, (1, LANES), 1)

    def across(at):
        return jnp.where((at >= rows) & (row_group > 0), at - every, at)

    matrices = row_matrices(taps, rows, every, across)
    halo_matrices = row_matrices(taps, rows, halo_rows, lambda at: across(at + rows))

    for s in range(2):

        def store(b, value, s=s):
            for g in range(rows // 8):
                at = pl.ds(8 * g * 2 * BLOCKS + s * BLOCKS + LEFT + b, 8, stride=2 * BLOCKS)
                out[at, :] = value[8 * g : 8 * g + 8]

        moved = Shifted(ints, s, [own, halo.at[:, :, : own.shape[2]]])
        overlap, lead, shift = moved.overlap, moved.lead, moved.shift
        mirror = jnp.broadcast_to((lead - 1 - lane) & (LANES - 1), (every, LANES))
        flipped = [
            jnp.take_along_axis(block_of([seam, seam_halo], s, j), mirror, axis=1, mode="promise_in_bounds")
            for j in range(LEFT)
        ]

        def blended(b, first, second):
            weight = jnp.clip((moved.column(b).astype(f32) + 0.5) / overlap.astype(f32), 0.0, 1.0)
            mine = jnp.where(moved.keep, first, second)
            other = jnp.where(lane < lead, flipped[min(max(-b, 0), 3)], flipped[min(max(-b - 1, 0), 3)])
            return -jnp.log(weight * mine + (1.0 - weight) * other)

        for b in range(-LEFT, 2, 2):
            parts = [moved.turned(b + i) for i in range(3)]
            logs = [blended(b + i, parts[i], parts[i + 1]) for i in range(2)]
            value = row_filter(matrices, jnp.concatenate(logs, axis=1))
            store(b, value[:, :LANES])
            store(b + 1, value[:, LANES:])

        rest = Shifted(ints, s, [halo])

        def pair(i, carry, s=s, store=store, rest=rest):
            b = 2 * i
            at = pl.ds(pl.multiple_of((b - 2) * LANES, 2 * LANES), 2 * LANES)
            value = early[s, :, at] + row_filter(halo_matrices, rest.plain_pair(b, width))
            store(b, value[:, :LANES])
            value = value[:, LANES:]
            last = b + 2 == width // LANES
            value = jnp.where(last & (lane == LANES - 1), rest.shift.astype(f32), value)
            value = jnp.where(last & (lane == LANES - 2) & (rest.shift > 1), rest.lead.astype(f32), value)
            store(b + 1, value)
            return carry

        lax.fori_loop(1, width // LANES // 2, pair, 0, unroll=15)


def times(a, b):
    return (a[0] * b[0] - a[1] * b[1], a[0] * b[1] + a[1] * b[0])


def dft(x, sign):
    n = len(x)
    if n == 1:
        return x
    even, odd = dft(x[0::2], sign), dft(x[1::2], sign)
    root = math.sqrt(0.5)
    first, second = [], []
    for k in range(n // 2):
        re, im = odd[k]
        if 4 * k == n:
            re, im = -sign * im, sign * re
        elif 8 * k == n:
            re, im = root * (re - sign * im), root * (im + sign * re)
        elif 8 * k == 3 * n:
            re, im = root * (-re - sign * im), root * (-im + sign * re)
        first.append((even[k][0] + re, even[k][1] + im))
        second.append((even[k][0] - re, even[k][1] - im))
    return first + second


def small_twist(value, power, sign):
    if power % OUTER == 0:
        return value
    angle = sign * 2.0 * math.pi * (power % OUTER) / OUTER
    return times(value, (np.float32(math.cos(angle)), np.float32(math.sin(angle))))


def sinogram_kernel(
    x, table, weights, out_hbm, out, field, mid_re, mid_im, rows, end_rows, sent
):
    gain_re, gain_im, twist_re, twist_im, end_u, end_v, ramp, _ = (
        table.at[OUTER * (k // 2) : OUTER * (k // 2 + 1), LANES * (k % 2) : LANES * (k % 2 + 1)] for k in range(8)
    )
    box = weights.at[: 2 * OUTER]
    forward, backward = ([weights.at[(at + k) * 2 * LANES - LANES : (at + k + 1) * 2 * LANES - LANES] for k in range(2)] for at in (1, 3))
    end_w = weights.at[5 * 2 * LANES - LANES :]
    half = out.shape[0] // 2
    lane = lax.broadcasted_iota(jnp.int32, (8, LANES), 1)

    def place(g, carry):
        sides = []
        for side in range(2):
            start = (side * half + 8 * g) * BLOCKS
            blocks = [x[pl.ds(start + k, 8, stride=BLOCKS), :] for k in range(BLOCKS)]
            last = blocks[-1]
            shift = last[:, LANES - 1 :]
            lead = jnp.where(shift > 1.5, last[:, LANES - 2 : LANES - 1], float(MIN_OVERLAP_OFFSET))
            hidden = (lane == LANES - 1) | ((lane == LANES - 2) & (shift > 1.5))
            blocks[-1] = jnp.where(hidden, 0.0, last)
            sides.append((blocks, shift.astype(jnp.int32), lead.astype(jnp.int32)))
        for side in range(2):
            mine, _, lead = sides[side]
            theirs, their_shift, _ = sides[1 - side]
            at = pl.ds(pl.multiple_of(side * half + 8 * g, 8), 8)
            spot = LANES - 1 + lead - their_shift - lane
            index = spot & (LANES - 1)
            jump = (spot >> 7) + 4
            mirrored = {}
            for k in range(OUTER // 2):
                mirrored[k] = jnp.take_along_axis(theirs[LEFT + k], index, axis=1, mode="promise_in_bounds")
            mirrored[-1] = mirrored[0]
            mirrored[OUTER // 2] = jnp.zeros((8, LANES), f32)
            for step in (1, 2, 4):
                moved = (jump & step) != 0
                top = OUTER // 2
                mirrored = {
                    k: jnp.where(moved, mirrored[min(k + step, top)], mirrored[k]) for k in mirrored
                }
            for c in range(OUTER // 2 - LEFT + 1):
                value = mirrored[OUTER // 2 - 5 - c]
                if c == OUTER // 2 - LEFT:
                    value = jnp.where(lane >= lead, mine[0], value)
                field[c, at, :] = value
            for k in range(1, BLOCKS):
                field[OUTER // 2 - LEFT + k, at, :] = mine[k]
        return carry

    lax.fori_loop(0, half // 8, place, 0, unroll=2)

    def highpass(i, carry):
        both = jnp.concatenate([field[2 * i], field[2 * i + 1]], axis=1)
        high, low = halves(both)
        sums = mxu(box[...], jnp.concatenate([high, low], axis=0))
        both = both - sums * np.float32(1.0 / ANGLE_TAPS)
        field[2 * i] = both[:, :LANES]
        field[2 * i + 1] = both[:, LANES:]
        return carry

    lax.fori_loop(0, OUTER // 2, highpass, 0, unroll=8)

    edge = lax.broadcasted_iota(jnp.int32, (1, LANES), 1) < LANES // 2
    border = [jnp.where(edge, field[0, at : at + half], field[OUTER - 1, at : at + half]) for at in (0, half)]
    tail_of = [table[4 * OUTER :, LANES * k : LANES * (k + 1)] for k in range(2)]
    tails = jnp.dot(border[0], tail_of[0], precision=lax.Precision.HIGHEST, preferred_element_type=f32)
    tails += jnp.dot(border[1], tail_of[1], precision=lax.Precision.HIGHEST, preferred_element_type=f32)
    end_rows[:, :LANES] = tails
    end_rows[:, LANES:] = pltpu.roll(tails, 2 * REACH, 1)

    def outer_forward(low_at, high_at, mid_re, mid_im, rows):
        for b in range(8):
            got = dft([(field[8 * a + b, low_at, :], field[8 * a + b, high_at, :]) for a in range(8)], -1.0)
            for d in range(8):
                mid_re[8 * d + b], mid_im[8 * d + b] = small_twist(got[d], d * b, -1.0)
        for d in range(8):
            got = dft([(mid_re[8 * d + b], mid_im[8 * d + b]) for b in range(8)], -1.0)
            for e in range(8):
                k = d + 8 * e
                re, im = times(got[e], (twist_re[k : k + 1, :], twist_im[k : k + 1, :]))
                rows[k, :, :LANES] = re
                rows[k, :, LANES:] = im

    def inner(low_at, rows):
        for part in range(2):
            n = OUTER // 2
            span = slice(part * n, (part + 1) * n)
            high, low = halves(rows[span].reshape(n * 8, 2 * LANES))
            spectrum = mxu(high, forward[0][...]) + mxu(low, forward[0][...]) + mxu(high, forward[1][...])
            spectrum = spectrum.reshape(n, 8, 2 * LANES)
            here = end_rows[low_at, :]
            tail = here[None, :, :LANES] * end_u[span][:, None, :] + here[None, :, LANES:] * end_v[span][:, None, :]
            tail = tail.reshape(n * 8, LANES)
            t_high = tail.astype(bf16).astype(f32)
            front = lax.broadcasted_iota(jnp.int32, (1, LANES), 1) < LANES // 2
            t_one = jnp.where(front, t_high, tail - t_high).astype(bf16)
            wrapped = mxu(jnp.concatenate([t_one, t_one], axis=1), end_w[...]).reshape(n, 8, 2 * LANES)
            g_re, g_im, r = gain_re[span][:, None, :], gain_im[span][:, None, :], ramp[span][:, None, :]
            re, im = times((spectrum[..., :LANES], spectrum[..., LANES:]), (g_re, g_im))
            re = re - r * wrapped[..., :LANES]
            im = im - r * wrapped[..., LANES:]
            high, low = halves(jnp.concatenate([re, im], axis=2).reshape(n * 8, 2 * LANES))
            signal = mxu(high, backward[0][...]) + mxu(low, backward[0][...]) + mxu(high, backward[1][...])
            signal = signal.reshape(n, 8, 2 * LANES)
            re, im = times(
                (signal[..., :LANES], signal[..., LANES:]), (twist_re[span][:, None, :], -twist_im[span][:, None, :])
            )
            rows[span, :, :LANES] = re
            rows[span, :, LANES:] = im

    def outer_backward(low_at, high_at, mid_re, mid_im, rows):
        for d in range(8):
            got = dft([(rows[d + 8 * e, :, :LANES], rows[d + 8 * e, :, LANES:]) for e in range(8)], 1.0)
            for b in range(8):
                mid_re[8 * d + b], mid_im[8 * d + b] = small_twist(got[b], d * b, 1.0)
        for b in range(8):
            got = dft([(mid_re[8 * d + b], mid_im[8 * d + b]) for d in range(8)], 1.0)
            for a in range(8):
                c = 8 * a + b
                out[low_at, c * LANES : (c + 1) * LANES] = got[a][0]
                out[high_at, c * LANES : (c + 1) * LANES] = got[a][1]

    def copies(g):
        for side in range(2):
            at = pl.ds(pl.multiple_of(side * half + 8 * g, 8), 8)
            yield pltpu.make_async_copy(out.at[at], out_hbm.at[at], sent.at[side, g])

    def filtered(i, carry):
        spots = []
        for j in range(TOGETHER):
            g = TOGETHER * i + j
            low_at = pl.ds(pl.multiple_of(8 * g, 8), 8)
            high_at = pl.ds(pl.multiple_of(half + 8 * g, 8), 8)
            spots.append((low_at, high_at, mid_re.at[j], mid_im.at[j], rows.at[j]))
        for spot in spots:
            outer_forward(*spot)
        for spot in spots:
            inner(spot[0], spot[4])
        for j, spot in enumerate(spots):
            outer_backward(*spot)
            for copy in copies(TOGETHER * i + j):
                copy.start()
        return carry

    lax.fori_loop(0, half // 8 // TOGETHER, filtered, 0)
    for g in range(half // 8):
        for copy in copies(g):
            copy.wait()


@functools.lru_cache(maxsize=None)
def tables(nproj):
    k1 = np.arange(OUTER)[:, None]
    l = np.arange(LANES)[None, :]
    angle = 2.0 * np.pi * (k1 * l % LENGTH) / LENGTH
    table = dict(twist_re=np.cos(angle), twist_im=-np.sin(angle))
    inner = 2.0 * np.pi * (np.arange(LANES)[:, None] * l % LANES) / LANES
    cos, sin = np.cos(inner), np.sin(inner)
    forward = np.block([[cos, -sin], [sin, cos]])
    backward = np.block([[cos, sin], [-sin, cos]])

    def two(w):
        high = w.astype(np.float32).astype(jnp.bfloat16)
        low = (w - high.astype(np.float64)).astype(np.float32).astype(jnp.bfloat16)
        return high, low

    table["forward"] = np.stack(two(forward))
    table["backward"] = np.stack(two(backward))
    columns = np.concatenate([np.arange(REACH), LENGTH - REACH + np.arange(REACH)])
    some = columns % LANES
    end_w = np.concatenate([forward[some], forward[LANES + some]], axis=0)
    high, low = two(end_w)
    table["end_w"] = np.concatenate([high, high, low, np.zeros_like(low)], axis=0)
    theta = 2.0 * np.pi * (k1 * columns[None, :] % LENGTH) / LENGTH
    table["end_u"] = np.tile(np.cos(theta), (1, 4))
    table["end_v"] = np.tile(np.concatenate([np.sin(theta), -np.sin(theta)], axis=1), (1, 2))
    tap_at = np.full((LANES, 2, 4, 2 * REACH), -1, np.int32)
    for i in range(REACH):
        for group in range(4):
            for t in range(TAPS):
                if LANES - REACH + i + t < LANES:
                    tap_at[LANES - REACH + i + t, group % 2, group, i] = t
                if i + t - 2 * REACH >= 0:
                    tap_at[i + t - 2 * REACH, group % 2, group, REACH + i] = t
    table["tap_at"] = tap_at.reshape(LANES, 2 * LANES)
    frequency = k1 + OUTER * l
    table["ramp"] = np.minimum(frequency, LENGTH - frequency) / (LENGTH / 2) / LENGTH
    lag = np.arange(TAPS) - REACH
    a = 2.0 * np.pi * (k1 * lag[None, :] % LENGTH) / LENGTH
    b = 2.0 * np.pi * (lag[:, None] * l % LANES) / LANES
    table["gain_left"] = np.stack(
        [np.concatenate([np.cos(a), -np.sin(a)], axis=1), np.concatenate([np.sin(a), np.cos(a)], axis=1)]
    )
    table["gain_right"] = np.concatenate([np.cos(b), np.sin(b)], axis=0)
    p = np.arange(nproj)
    gap = (p[:, None] - p[None, :]) % nproj
    near = (np.minimum(gap, nproj - gap) <= ANGLE_TAPS // 2).astype(np.float32).astype(jnp.bfloat16)
    table["box"] = np.concatenate([near, near], axis=1)
    pairs = (("twist_re", "twist_im"), ("end_u", "end_v"), ("ramp", "ramp"))
    fixed = np.block([[table[k] for k in pair] for pair in pairs]).astype(np.float32)
    weights = np.concatenate([table["box"], *table["forward"], *table["backward"], table["end_w"]], axis=0)
    gain = [table[k].astype(np.float32) for k in ("gain_left", "gain_right")]
    return fixed, weights, gain, table["tap_at"]


def vmem_spec():
    return pl.BlockSpec(memory_space=pltpu.VMEM)


def hbm_spec():
    return pl.BlockSpec(memory_space=pl.ANY)


def smem_spec():
    return pl.BlockSpec(memory_space=pltpu.SMEM)


def early_side(ints, taps, projections):
    per, rows, width = projections.shape
    shape = jax.ShapeDtypeStruct((per, rows, width - 2 * LANES), f32)
    return pl.pallas_call(
        early_kernel,
        out_shape=shape,
        in_specs=[smem_spec(), smem_spec(), vmem_spec()],
        out_specs=vmem_spec(),
        compiler_params=pltpu.CompilerParams(vmem_limit_bytes=24 * 1024 * 1024),
        cost_estimate=pl.CostEstimate(flops=12 * per * rows * rows * width, bytes_accessed=8 * per * rows * width, transcendentals=per * rows * width),
        name="early",
    )(ints, taps, projections)


def source_side(ints, taps, early, projections, halo, seam, seam_halo):
    per, rows, _ = projections.shape
    return pl.pallas_call(
        source_kernel,
        grid=(1,),
        out_shape=jax.ShapeDtypeStruct((rows * per * BLOCKS, LANES), f32),
        in_specs=[smem_spec(), smem_spec(), vmem_spec(), pl.BlockSpec((per, rows, 8 * LANES), lambda i: (0, 0, 0))]
        + [vmem_spec()] * 3,
        out_specs=vmem_spec(),
        compiler_params=pltpu.CompilerParams(vmem_limit_bytes=24 * 1024 * 1024),
        name="source",
    )(ints, taps, early, projections, halo, seam, seam_halo)


def sinogram_side(got, taps):
    nproj = got.shape[0] // BLOCKS
    fixed, weights, (gain_left, gain_right), tap_at = tables(nproj)
    left = (gain_left * jnp.tile(taps[0], 2)).reshape(2 * OUTER, 2 * TAPS)
    gain = jnp.dot(left, gain_right, precision=lax.Precision.HIGHEST) * jnp.tile(fixed[2 * OUTER :, :LANES], (2, 1))
    ends = jnp.zeros(tap_at.shape, f32)
    for k in range(TAPS):
        ends = jnp.where(tap_at == k, taps[0, k], ends)
    table = jnp.concatenate([jnp.concatenate([gain[:OUTER], gain[OUTER:]], axis=1), fixed, ends], axis=0)
    return pl.pallas_call(
        sinogram_kernel,
        out_shape=jax.ShapeDtypeStruct((nproj, LENGTH), f32),
        in_specs=[vmem_spec()] * 3,
        out_specs=hbm_spec(),
        scratch_shapes=[
            pltpu.VMEM((nproj, LENGTH), f32),
            pltpu.VMEM((OUTER, nproj, LANES), f32),
            pltpu.VMEM((TOGETHER, OUTER, 8, LANES), f32),
            pltpu.VMEM((TOGETHER, OUTER, 8, LANES), f32),
            pltpu.VMEM((TOGETHER, OUTER, 8, 2 * LANES), f32),
            pltpu.VMEM((nproj // 2, 2 * LANES), f32),
            pltpu.SemaphoreType.DMA((2, nproj // 16)),
        ],
        compiler_params=pltpu.CompilerParams(vmem_limit_bytes=28 * 1024 * 1024),
        name="sinogram",
    )(got, table, jnp.asarray(weights))


def local(projections, correlation, offset, smooth_taps):
    ang, row = lax.axis_size("ang"), lax.axis_size("row")
    here = lax.axis_index("row")
    per, rows, width = projections.shape
    nproj = per * ang
    seam_cols = LEFT * LANES

    halo = lax.dynamic_slice_in_dim(projections, jnp.where(here == 0, rows - REACH, 0), REACH, axis=1)
    half_turn = [(i, (i + ang // 2) % ang) for i in range(ang)]
    across = [(i, 1 - i) for i in range(row)]
    both = [(a * row + r, b * row + s) for a, b in half_turn for r, s in across]
    seam_halo = lax.ppermute(halo[:, :, :seam_cols], ("ang", "row"), both)
    seam = lax.ppermute(projections[:, :, :seam_cols], "ang", half_turn)
    halo = lax.ppermute(halo, "row", across)

    taps = smooth_taps / jnp.sum(smooth_taps, axis=1, keepdims=True)
    ints = jnp.concatenate([correlation, offset, here[None].astype(jnp.int32)])
    early = early_side(ints, taps, projections)
    sent = source_side(ints, taps, early, projections, halo, seam, seam_halo)
    got = lax.all_to_all(sent.reshape(rows, per * BLOCKS, LANES), "ang", split_axis=0, concat_axis=0, tiled=True)
    return sinogram_side(got.reshape(nproj * BLOCKS, LANES), taps)[None, None]


def solution(mesh):
    P = jax.sharding.PartitionSpec
    placed = (P("ang", "row", None), P("ang"), P("ang"), P())
    return jax.shard_map(
        local, mesh=mesh, in_specs=placed, out_specs=P("row", "ang", None, None), check_vma=False
    )
```
